128 devices in a mesh: dp: 2 (over core), ctx: 16 (over y, x), head: 4 (over z).
Axes of the slice: x: 4, y: 4, z: 4, core: 2. Of those that a mesh axis runs over, the one named last changes fastest.
Arguments:
- group_queries: bfloat16 [4, 1024, 7168], P('dp', 'ctx', 'head'), parts along dimension 0, may hold values from -15 to 15
- group_keys: bfloat16 [4, 1024, 7168], P('dp', 'ctx', 'head'), parts along dimension 0, may hold values from -6 to 6
- group_values: bfloat16 [4, 1024, 7168], P('dp', 'ctx', 'head'), parts along dimension 0, may hold values from -6 to 6
- cache_keys: bfloat16 [4, 16384, 7168], P('dp', 'ctx', 'head'), parts along dimension 0, may hold values from -6 to 6
- cache_values: bfloat16 [4, 16384, 7168], P('dp', 'ctx', 'head'), parts along dimension 0, may hold values from -6 to 6
- cache_lengths: int32 [4], P('dp'), parts along dimension 0, may hold values from 4096 to 16384, as said below
- mamba_x: bfloat16 [4, 1024, 7168], P('dp', 'ctx', 'head'), parts along dimension 0, may hold values from -6 to 6
- mamba_bc: bfloat16 [4, 1024, 128], P('dp', 'ctx'), parts along dimension 0, may hold values from -1.5 to 1.5
- mamba_dt: bfloat16 [4, 1024, 112], P('dp', 'ctx', 'head'), parts along dimension 0, may hold values from -2.5 to 2.5
- conv_state_x: bfloat16 [4, 3, 7168], P('dp', None, 'head'), parts along dimension 0, may hold values from -6 to 6
- conv_state_bc: bfloat16 [4, 3, 128], P('dp'), parts along dimension 0, may hold values from -1.5 to 1.5
- conv_weight_x: float32 [4, 7168], P(None, 'head'), may hold values from -3 to 3
- conv_bias_x: float32 [7168], P('head'), may hold values from -3 to 3
- conv_weight_bc: float32 [4, 128], replicated, may hold values from -3 to 3
- conv_bias_bc: float32 [128], replicated, may hold values from -0.6 to 0.6
- dt_bias: float32 [112], P('head'), may hold values from 0 to 1
- a_log: float32 [112], P('head'), as said below
- skip_d: float32 [112], P('head'), may hold values from 0.5 to 1.5
- ssm_state: float32 [4, 112, 64, 64], P('dp', 'head'), parts along dimension 0, may hold values from -12 to 12
Outputs:
- attention_out: bfloat16 [4, 1024, 7168], P('dp', 'ctx', 'head'), parts along dimension 0
- mamba_out: bfloat16 [4, 1024, 7168], P('dp', 'ctx', 'head'), parts along dimension 0
The draws below stay inside these ranges and needn't reach their ends.
There are 2 independent parts, one for each index of `dp`. The reference program is written for one: setup_inputs(seed, part) draws one part's arguments, and reference() takes and returns one part's arrays. A program takes and returns all parts, laid end to end along the dimension named above; an argument that names none is the same for every part. Nothing has to cross between parts.
Inputs may be any that keep to these rules, and one draw needn't show every extreme that they name: `cache_lengths`: each request's count of valid cache positions; some request has all 16384. `a_log`: log of each head's decay rate per unit of step size.
All inputs are finite; a program needn't handle non-finite values.
Results may differ from the reference program's by a relative error of at most 0.005.
Values may be sent and summed in bfloat16 or wider, within the bound.
No kernel may reach another device: no remote copies, remote signals or barrier semaphores. Data moves between devices by JAX's collectives and lax.ppermute only.
A program may use at most 256 MiB of HBM per device.

```python
import math
import jax
import jax.numpy as jnp
from jax import lax

HQ = 32
HD = 224
MH = 112
MP = 64
NS = 64
KW = 4
REQ = 2
GROUP = 1024
CACHE = 16384


def draw_group_queries(key, part):
    key = jax.random.fold_in(key, 1)
    sample = 2.5 * jax.random.normal(key, (REQ, GROUP, HQ * HD), jnp.float32)
    return jnp.clip(sample, -15.0, 15.0).astype(jnp.bfloat16)


def draw_cache_keys(key, part):
    key = jax.random.fold_in(key, 2)
    sample = jax.random.normal(key, (REQ, CACHE, HQ * HD), jnp.float32)
    return jnp.clip(sample, -6.0, 6.0).astype(jnp.bfloat16)


def draw_cache_lengths(key, part):
    key = jax.random.fold_in(key, 3)
    length_key, pick_key = jax.random.split(key)
    lengths = jax.random.randint(length_key, (REQ,), CACHE // 4, CACHE + 1)
    full_request = jax.random.randint(pick_key, (), 0, REQ)
    return jnp.where(jnp.arange(REQ, dtype=jnp.int32) == full_request, CACHE, lengths).astype(jnp.int32)


def draw_a_log(key, part):
    key = jax.random.fold_in(key, 4)
    kind_key, slow_key, fast_key = jax.random.split(key, 3)
    slow_share = 0.5
    slow_heads = jax.random.bernoulli(kind_key, slow_share, (MH,))
    slow_rate = 2.0 / GROUP * jnp.exp(jax.random.uniform(slow_key, (MH,), jnp.float32, math.log(0.05), 0.0))
    fast_rate = jnp.exp(jax.random.uniform(fast_key, (MH,), jnp.float32, math.log(1.0 / 50.0), math.log(1.0 / 30.0)))
    return jnp.log(jnp.where(slow_heads, slow_rate, fast_rate)).astype(jnp.float32)


def steps_of(rng, extent, pieces, smallest, high):
    level, own = 1.0, jax.random.fold_in(rng, 6)
    for axis_at, parts in pieces:
        steps = jnp.exp(jax.random.uniform(jax.random.fold_in(own, axis_at), (parts,), jnp.float32, smallest / len(pieces), high / len(pieces)))
        level = level * jnp.repeat(steps, extent[axis_at] // parts).reshape([-1 if axis == axis_at else 1 for axis in range(len(extent))])
    return level


def noise(rng, dims, spread, reach, cuts=(), kind=jnp.bfloat16):
    level = steps_of(rng, dims, cuts, -0.22, 0.18) if cuts else 1.0
    values = jax.random.normal(rng, dims, jnp.float32) * spread * level
    return jnp.minimum(jnp.maximum(values, -reach), reach).astype(kind)


def setup_inputs(seed: int = 0, part: int = 0) -> dict:
    splits = jax.random.split(jax.random.key(seed), 20)
    part_splits = jax.random.split(jax.random.fold_in(splits[19], part), 20)
    group_queries = draw_group_queries(jax.random.fold_in(jax.random.fold_in(splits[19], part), 71), part)
    group_keys = noise(part_splits[1], (REQ, GROUP, HQ * HD), 1.0, 6.0, ((1, 16), (2, 4)))
    group_values = noise(part_splits[2], (REQ, GROUP, HQ * HD), 1.0, 6.0, ((1, 16), (2, 4)))
    cache_keys = draw_cache_keys(jax.random.fold_in(jax.random.fold_in(splits[19], part), 71), part)
    cache_values = noise(part_splits[4], (REQ, CACHE, HQ * HD), 1.0, 6.0, ((1, 16), (2, 4)))
    cache_lengths = draw_cache_lengths(jax.random.fold_in(jax.random.fold_in(splits[19], part), 71), part)
    mamba_x = noise(part_splits[6], (REQ, GROUP, MH * MP), 1.0, 6.0, ((1, 16), (2, 4)))
    mamba_bc = noise(part_splits[7], (REQ, GROUP, 2 * NS), 0.25, 1.5, ((1, 16),))
    mamba_dt = noise(part_splits[8], (REQ, GROUP, MH), 0.5, 2.5, ((1, 16), (2, 4)))
    conv_state_x = noise(part_splits[9], (REQ, KW - 1, MH * MP), 1.0, 6.0, ((2, 4),))
    conv_state_bc = noise(part_splits[10], (REQ, KW - 1, 2 * NS), 0.25, 1.5)
    conv_weight_x = noise(splits[11], (KW, MH * MP), KW ** -0.5, 3.0, ((1, 4),), jnp.float32)
    conv_bias_x = noise(splits[12], (MH * MP,), 0.5, 3.0, ((0, 4),), jnp.float32)
    conv_weight_bc = noise(splits[13], (KW, 2 * NS), KW ** -0.5, 3.0, (), jnp.float32)
    conv_bias_bc = noise(splits[14], (2 * NS,), 0.1, 0.6, (), jnp.float32)
    dt_bias = jnp.clip(1.0 * jax.random.uniform(splits[15], (MH,), jnp.float32) ** steps_of(splits[15], (MH,), ((0, 4),), -0.2, 0.2), 0.0, 1.0)
    a_log = draw_a_log(jax.random.fold_in(splits[19], 71), part)
    skip_d = jnp.clip(0.5 + 1.0 * jax.random.uniform(splits[17], (MH,), jnp.float32) ** steps_of(splits[17], (MH,), ((0, 4),), -0.2, 0.2), 0.5, 1.5)
    ssm_state = noise(part_splits[18], (REQ, MH, MP, NS), 2.0, 12.0, ((1, 4),), jnp.float32)
    return {"group_queries": group_queries, "group_keys": group_keys, "group_values": group_values, "cache_keys": cache_keys, "cache_values": cache_values, "cache_lengths": cache_lengths, "mamba_x": mamba_x, "mamba_bc": mamba_bc, "mamba_dt": mamba_dt, "conv_state_x": conv_state_x, "conv_state_bc": conv_state_bc, "conv_weight_x": conv_weight_x, "conv_bias_x": conv_bias_x, "conv_weight_bc": conv_weight_bc, "conv_bias_bc": conv_bias_bc, "dt_bias": dt_bias, "a_log": a_log, "skip_d": skip_d, "ssm_state": ssm_state}


NEG_FILL = -1e+30

def causal_conv(previous, current, conv_taps, conv_bias):
    joined = jnp.concatenate([previous, current], axis=1).astype(jnp.float32)
    token_count = current.shape[1]
    acc_total = jnp.zeros(current.shape, jnp.float32) + conv_bias.astype(jnp.float32)[None, None, :]
    for offset in range(conv_taps.shape[0]):
        acc_total = acc_total + conv_taps[offset].astype(jnp.float32)[None, None, :] * joined[:, offset:offset + token_count, :]
    return jax.nn.silu(acc_total)

def reference(group_queries, group_keys, group_values, cache_keys, cache_values, cache_lengths, mamba_x, mamba_bc, mamba_dt, conv_state_x, conv_state_bc, conv_weight_x, conv_bias_x, conv_weight_bc, conv_bias_bc, dt_bias, a_log, skip_d, ssm_state):
    score_scale = 1.0 / math.sqrt(HD)
    query_index = jnp.arange(GROUP, dtype=jnp.int32)
    cache_index = jnp.arange(CACHE, dtype=jnp.int32)
    causal_mask = query_index[None, :] <= query_index[:, None]
    outputs_list = []
    for request in range(REQ):
        cache_ok = jnp.broadcast_to(cache_index[None, :] < cache_lengths[request], (GROUP, CACHE))
        allowed = jnp.concatenate([cache_ok, causal_mask], axis=1)
        query_all = group_queries[request].reshape(GROUP, HQ, HD)
        key_all = jnp.concatenate([cache_keys[request], group_keys[request]], axis=0).reshape(CACHE + GROUP, HQ, HD)
        value_all = jnp.concatenate([cache_values[request], group_values[request]], axis=0).reshape(CACHE + GROUP, HQ, HD)

        def one_head(head_number):
            query_head = lax.dynamic_index_in_dim(query_all, head_number, 1, keepdims=False)
            key_head = lax.dynamic_index_in_dim(key_all, head_number, 1, keepdims=False)
            value_head = lax.dynamic_index_in_dim(value_all, head_number, 1, keepdims=False)
            scores = jnp.dot(query_head, key_head.T, preferred_element_type=jnp.float32) * score_scale
            masked = jnp.where(allowed, scores, NEG_FILL)
            row_top = lax.optimization_barrier(jnp.max(masked, axis=1))
            weights = jnp.where(allowed, jnp.exp(masked - row_top[:, None]), 0.0)
            row_total = lax.optimization_barrier(jnp.sum(weights, axis=1))
            summed = jnp.dot(weights, value_head.astype(jnp.float32), precision=lax.Precision.HIGHEST, preferred_element_type=jnp.float32)
            return (summed / row_total[:, None]).astype(jnp.bfloat16)
        head_outputs = lax.map(one_head, jnp.arange(HQ, dtype=jnp.int32))
        outputs_list.append(head_outputs.transpose(1, 0, 2).reshape(GROUP, HQ * HD))
    attention_out = jnp.stack(outputs_list)
    inner_act = causal_conv(conv_state_x, mamba_x, conv_weight_x, conv_bias_x)
    mixed_bc = causal_conv(conv_state_bc, mamba_bc, conv_weight_bc, conv_bias_bc)
    inputs_b = mixed_bc[..., :NS]
    outputs_c = mixed_bc[..., NS:]
    inner_heads = inner_act.reshape(REQ, GROUP, MH, MP)
    step_size = jax.nn.softplus(mamba_dt.astype(jnp.float32) + dt_bias[None, None, :])
    decay = jnp.exp(-jnp.exp(a_log)[None, None, :] * step_size)

    def advance(state, item):
        inner_step, b_step, c_step, size_step, decay_step = item
        state = decay_step[:, :, None, None] * state + (size_step[:, :, None] * inner_step)[..., None] * b_step[:, None, None, :]
        return (state, lax.optimization_barrier(jnp.sum(state * c_step[:, None, None, :], axis=3)))
    sequence_items = (inner_heads.transpose(1, 0, 2, 3), inputs_b.transpose(1, 0, 2), outputs_c.transpose(1, 0, 2), step_size.transpose(1, 0, 2), decay.transpose(1, 0, 2))
    final_state, readout = lax.scan(advance, ssm_state, sequence_items)
    result = readout.transpose(1, 0, 2, 3) + skip_d[None, None, :, None] * inner_heads
    mamba_out = result.reshape(REQ, GROUP, MH * MP).astype(jnp.bfloat16)
    return (attention_out, mamba_out)
```

```python
import functools
import math

import jax
import jax.numpy as jnp
from jax import lax
from jax.experimental import pallas as pl
from jax.experimental.pallas import tpu as pltpu
from jax.sharding import PartitionSpec as P

HD = 224
PAD = 256
L_LANE = 224
M_LANE = 226
NEG_FILL = -1e30
EMPTY_TOP = -8192.0
HIGHEST = lax.Precision.HIGHEST
BF = jnp.bfloat16
F32 = jnp.float32
SIDE = 4
VMEM_LIMIT = 56 * 1024 * 1024


def params(**extra):
    return pltpu.CompilerParams(vmem_limit_bytes=VMEM_LIMIT, **extra)


def shifted(value, dy, dx):
    pairs = [
        (y * SIDE + x, ((y + dy) % SIDE) * SIDE + (x + dx) % SIDE)
        for y in range(SIDE)
        for x in range(SIDE)
    ]
    return lax.ppermute(value, "ctx", pairs)


def along(axis):
    if axis == "x":
        return lambda value, step: shifted(value, 0, step)
    return lambda value, step: shifted(value, step, 0)


def pad_kernel(info, k_ref, gk_ref, v_ref, gv_ref, ko_ref, vo_ref):
    request = pl.program_id(0)
    rows = k_ref.shape[1]
    group_rows = gk_ref.shape[1]
    heads = ko_ref.shape[1]
    first = info[0] * rows
    length = info[1 + request]
    lane = lax.broadcasted_iota(jnp.int32, (rows, PAD - HD), 1)
    row = lax.broadcasted_iota(jnp.int32, (rows, PAD - HD), 0)
    cache_bias = jnp.where((lane == 0) & (first + row >= length), NEG_FILL, 0.0).astype(BF)
    group_bias = jnp.zeros((group_rows, PAD - HD), BF)
    ones = jnp.where(lane == 0, 1.0, 0.0).astype(BF)
    for h in range(heads):
        window = slice(h * HD, (h + 1) * HD)
        ko_ref[0, h, :rows, :] = jnp.concatenate([k_ref[0, :, window], cache_bias], axis=1)
        ko_ref[0, h, rows:, :] = jnp.concatenate([gk_ref[0, :, window], group_bias], axis=1)
        vo_ref[0, h, :rows, :] = jnp.concatenate([v_ref[0, :, window], ones], axis=1)
        vo_ref[0, h, rows:, :] = jnp.concatenate([gv_ref[0, :, window], ones[:group_rows]], axis=1)


def padded_cache(info, cache_keys, group_keys, cache_values, group_values):
    requests, rows, width = cache_keys.shape
    group_rows = group_keys.shape[1]
    heads = width // HD
    part = heads // 2
    total = rows + group_rows
    wide = pl.BlockSpec((1, rows, part * HD), lambda r, g, s: (r, 0, g))
    small = pl.BlockSpec((1, group_rows, part * HD), lambda r, g, s: (r, 0, g))
    out = pl.BlockSpec((1, part, total, PAD), lambda r, g, s: (r, g, 0, 0))
    shape = jax.ShapeDtypeStruct((requests, heads, total, PAD), BF)
    return pl.pallas_call(
        pad_kernel,
        grid_spec=pltpu.PrefetchScalarGridSpec(
            num_scalar_prefetch=1,
            grid=(requests, 2),
            in_specs=[wide, small, wide, small],
            out_specs=[out, out],
        ),
        out_shape=[shape, shape],
        compiler_params=params(),
        cost_estimate=pl.CostEstimate(flops=0, bytes_accessed=33_000_000, transcendentals=0),
        name="pad_cache",
    )(info, cache_keys, group_keys, cache_values, group_values)


def attend_kernel(counts, info, *refs):
    n0, n1 = counts
    q0_refs, q1_refs = refs[:n0], refs[n0 : n0 + n1]
    k_ref, v_ref, out0_ref, out1_ref, qs_ref = refs[n0 + n1 :]
    request = pl.program_id(0)
    step = pl.program_id(1)
    heads, rows, _ = qs_ref.shape
    here = k_ref.shape[1]
    total = k_ref.shape[2]
    block = 64
    cached = total - block

    def fill(q_refs):
        at = 0
        for ref in q_refs:
            count = ref.shape[0]
            lane = lax.broadcasted_iota(jnp.int32, (count, PAD - HD), 1)
            ones = jnp.where(lane == 0, 1.0, 0.0).astype(BF)
            for h in range(heads):
                qs_ref[h, at : at + count, :] = jnp.concatenate(
                    [ref[:, h * HD : (h + 1) * HD], ones], axis=1
                )
            at += count

    @pl.when((step == 0) & (request == 0))
    def _():
        fill(q0_refs)

    @pl.when((step == 0) & (request == 1))
    def _():
        fill(q1_refs)

    scale = math.log2(math.e) / math.sqrt(HD)
    blocks = rows // block
    position = info[0]

    def one(out_ref, base):
        row = lax.broadcasted_iota(jnp.int32, (block, block), 0)
        col = lax.broadcasted_iota(jnp.int32, (block, block), 1) + position * block
        masks = []
        for b in range(blocks):
            masks.append(col <= row + info[base + b] * block)
        allowed = jnp.concatenate(masks, axis=0)
        lane = lax.broadcasted_iota(jnp.int32, (rows, PAD), 1)
        for i in range(here):
            q = qs_ref[step * here + i]
            scores = lax.dot_general(
                q, k_ref[0, i, :cached, :], (((1,), (1,)), ((), ())), preferred_element_type=F32
            )
            tail = lax.dot_general(
                q, k_ref[0, i, cached:, :], (((1,), (1,)), ((), ())), preferred_element_type=F32
            )
            tail = jnp.where(allowed, tail, NEG_FILL)
            top = jnp.maximum(
                jnp.max(scores, axis=1, keepdims=True), jnp.max(tail, axis=1, keepdims=True)
            )
            top = jnp.round(jnp.maximum(top * scale, EMPTY_TOP)).astype(BF).astype(F32)
            p_scores = jnp.exp2(scores * scale - top).astype(BF)
            p_tail = jnp.exp2(tail * scale - top).astype(BF)
            summed = jnp.dot(p_scores, v_ref[0, i, :cached, :], preferred_element_type=F32)
            summed = summed + jnp.dot(p_tail, v_ref[0, i, cached:, :], preferred_element_type=F32)
            summed = jnp.where(lane == M_LANE, top, summed)
            out_ref[:, i * PAD : (i + 1) * PAD] = summed.astype(BF)

    @pl.when(request == 0)
    def _():
        one(out0_ref, 1)

    @pl.when(request == 1)
    def _():
        one(out1_ref, 1 + blocks)


def attend(info, q0, q1, keys, values):
    requests, heads, total, _ = keys.shape
    rows = sum(q.shape[0] for q in q0)
    here = 2
    steps = heads // here
    kv = pl.BlockSpec((1, here, total, PAD), lambda r, g, s: (r, g, 0, 0))
    whole = [pl.BlockSpec(q.shape, lambda r, g, s: (0, 0)) for q in (*q0, *q1)]
    out0 = pl.BlockSpec((rows, here * PAD), lambda r, g, s: (0, jnp.where(r == 0, g, steps - 1)))
    out1 = pl.BlockSpec((rows, here * PAD), lambda r, g, s: (0, jnp.where(r == 0, 0, g)))
    shape = jax.ShapeDtypeStruct((rows, heads * PAD), BF)
    work = requests * heads * rows * total
    return pl.pallas_call(
        functools.partial(attend_kernel, (len(q0), len(q1))),
        grid_spec=pltpu.PrefetchScalarGridSpec(
            num_scalar_prefetch=1,
            grid=(requests, steps),
            in_specs=[*whole, kv, kv],
            out_specs=[out0, out1],
            scratch_shapes=[pltpu.VMEM((heads, rows, PAD), BF)],
        ),
        out_shape=[shape, shape],
        compiler_params=params(),
        cost_estimate=pl.CostEstimate(
            flops=4 * work * PAD, bytes_accessed=18_000_000, transcendentals=work
        ),
        name="attend",
    )(info, *q0, *q1, keys, values)


def merged(parts):
    tops = [part[:, M_LANE : M_LANE + 1] for part in parts]
    top = functools.reduce(jnp.maximum, tops)
    summed = sum(part * jnp.exp2(own - top) for part, own in zip(parts, tops))
    return summed, top


def merge_kernel(count, *refs):
    out_ref = refs[count]
    heads = out_ref.shape[1] // PAD
    lane = lax.broadcasted_iota(jnp.int32, (out_ref.shape[0], PAD), 1)
    for h in range(heads):
        window = slice(h * PAD, (h + 1) * PAD)
        summed, top = merged([ref[:, window].astype(F32) for ref in refs[:count]])
        out_ref[:, window] = jnp.where(lane == M_LANE, top, summed).astype(BF)


def merge(parts):
    rows, width = parts[0].shape
    tile = 64
    spec = pl.BlockSpec((tile, width), lambda i: (i, 0))
    return pl.pallas_call(
        functools.partial(merge_kernel, len(parts)),
        grid=(rows // tile,),
        in_specs=[spec] * len(parts),
        out_specs=spec,
        out_shape=jax.ShapeDtypeStruct((rows, width), BF),
        compiler_params=params(),
        cost_estimate=pl.CostEstimate(
            flops=rows * width * 8, bytes_accessed=rows * width * 10, transcendentals=0
        ),
        name="merge",
    )(*parts)


def finish_kernel(count, *refs):
    out_ref = refs[2 * count]
    heads = out_ref.shape[2] // HD
    for r in range(2):
        done = []
        for h in range(heads):
            window = slice(h * PAD, (h + 1) * PAD)
            summed, _ = merged([ref[:, window].astype(F32) for ref in refs[r * count : (r + 1) * count]])
            done.append((summed / summed[:, L_LANE : L_LANE + 1])[:, :HD])
        out_ref[r] = jnp.concatenate(done, axis=1).astype(BF)


def finish(parts0, parts1):
    rows, width = parts0[0].shape
    heads = width // PAD
    return pl.pallas_call(
        functools.partial(finish_kernel, len(parts0)),
        out_shape=jax.ShapeDtypeStruct((2, rows, heads * HD), BF),
        compiler_params=params(),
        cost_estimate=pl.CostEstimate(
            flops=rows * width * 16, bytes_accessed=rows * width * 20, transcendentals=0
        ),
        name="finish",
    )(*parts0, *parts1)


def pack_kernel(x_ref, dt_ref, bc_ref, out_ref):
    rows = x_ref.shape[1]
    heads = dt_ref.shape[2]
    for r in range(2):
        extra = jnp.concatenate([dt_ref[r], jnp.zeros((rows, PAD - HD - heads), BF)], axis=1)
        for c in range(8):
            out_ref[r * 8 + c, :, :PAD] = jnp.concatenate(
                [x_ref[r, :, c * HD : (c + 1) * HD], extra], axis=1
            )
            out_ref[r * 8 + c, :, PAD:] = bc_ref[r]


def unpack_kernel(in_ref, out_ref):
    for r in range(2):
        out_ref[r] = jnp.concatenate(
            [in_ref[r * 8 + c].astype(F32)[:, :HD] for c in range(8)], axis=1
        ).astype(BF)


def scan_kernel(info, data_ref, par_ref, bcpar_ref, headpar_ref, state_ref, out_ref, xs_ref, bcs_ref):
    tokens = data_ref.shape[0]
    chunk = 128
    start = info[0]
    first_head = (7 * start) // 2
    xs_ref[0:8, :] = jnp.concatenate(
        [jnp.zeros((5, PAD), F32), par_ref[0:3, :]], axis=0
    )
    bcs_ref[0:8, :] = jnp.concatenate([jnp.zeros((5, 128), F32), bcpar_ref[0:3, :]], axis=0)
    xs_ref[8:, :] = data_ref[:, :PAD].astype(F32)
    bcs_ref[8:, :] = data_ref[:, PAD:].astype(F32)

    lane = lax.broadcasted_iota(jnp.int32, (8, PAD), 1) + start * HD
    head = lax.broadcasted_iota(jnp.int32, (8, PAD), 0) + first_head
    spread = (lane // 64 == head).astype(F32)
    pick = (
        lax.broadcasted_iota(jnp.int32, (128, 8), 0)
        == lax.broadcasted_iota(jnp.int32, (128, 8), 1) + (HD - 128) + first_head
    ).astype(F32)
    headpar = headpar_ref[...]
    dt_bias, rate, skip = headpar[0:1], jnp.exp(headpar[1:2]), headpar[2:3]
    skip_wide = jnp.dot(skip, spread, precision=HIGHEST, preferred_element_type=F32)
    row = lax.broadcasted_iota(jnp.int32, (chunk, chunk), 0)
    col = lax.broadcasted_iota(jnp.int32, (chunk, chunk), 1)
    lower = row >= col
    lower_f = lower.astype(F32)
    masks = [spread[h : h + 1] for h in range(4)]
    state = state_ref[...].T
    for c in range(tokens // chunk):
        at = c * chunk
        x = jnp.zeros((chunk, PAD), F32) + par_ref[7:8, :]
        bc = jnp.zeros((chunk, 128), F32) + bcpar_ref[7:8, :]
        for i in range(4):
            x = x + par_ref[3 + i : 4 + i, :] * xs_ref[at + 5 + i : at + 5 + i + chunk, :]
            bc = bc + bcpar_ref[3 + i : 4 + i, :] * bcs_ref[at + 5 + i : at + 5 + i + chunk, :]
        x = x * jax.nn.sigmoid(x)
        bc = bc * jax.nn.sigmoid(bc)
        b, o = bc[:, :64], bc[:, 64:]
        raw = xs_ref[at + 8 : at + 8 + chunk, 128:]
        size = jnp.dot(raw, pick, precision=HIGHEST, preferred_element_type=F32) + dt_bias
        size = jnp.maximum(size, 0.0) + jnp.log1p(jnp.exp(-jnp.abs(size)))
        run = jnp.dot(lower_f, -rate * size, precision=HIGHEST, preferred_element_type=F32)
        run_t = run.T
        wide = jnp.dot(
            jnp.concatenate([size, run], axis=0), spread, precision=HIGHEST, preferred_element_type=F32
        )
        size_wide, run_wide = wide[:chunk], wide[chunk:]
        xdt = x * size_wide
        cross = lax.dot_general(
            o, b, (((1,), (1,)), ((), ())), precision=HIGHEST, preferred_element_type=F32
        )
        pieces, mixes = [], []
        for h in range(4):
            gap = run[:, h : h + 1] - run_t[h : h + 1, :]
            mixes.append((jnp.exp(jnp.where(lower, gap, NEG_FILL)) * cross).astype(BF))
            pieces.append((xdt * masks[h]).astype(BF))
        y = jnp.dot(
            jnp.concatenate(mixes, axis=1), jnp.concatenate(pieces, axis=0), preferred_element_type=F32
        )
        y = y + jnp.exp(run_wide) * jnp.dot(o, state, precision=HIGHEST, preferred_element_type=F32)
        last = run_wide[chunk - 1 : chunk]
        state = state * jnp.exp(last) + lax.dot_general(
            b,
            xdt * jnp.exp(last - run_wide),
            (((0,), (0,)), ((), ())),
            precision=HIGHEST,
            preferred_element_type=F32,
        )
        out_ref[at : at + chunk, :] = (y + skip_wide * x).astype(BF)


def state_space(
    position, mamba_x, mamba_bc, mamba_dt, conv_state_x, conv_state_bc, conv_weight_x, conv_bias_x,
    conv_weight_bc, conv_bias_bc, dt_bias, a_log, skip_d, ssm_state,
):
    rows = mamba_x.shape[1]
    request, start = position // 8, position % 8
    packed = pl.pallas_call(
        pack_kernel,
        out_shape=jax.ShapeDtypeStruct((16, rows, PAD + 128), BF),
        compiler_params=params(),
        name="pack",
    )(mamba_x, mamba_dt, mamba_bc)
    mine = lax.all_to_all(packed, "ctx", 0, 0, tiled=True).reshape(16 * rows, PAD + 128)

    def at_request(value):
        return lax.dynamic_index_in_dim(value, request, 0, keepdims=False)

    par = jnp.concatenate([at_request(conv_state_x).astype(F32), conv_weight_x, conv_bias_x[None]], axis=0)
    par = jnp.pad(lax.dynamic_slice_in_dim(par, start * HD, HD, 1), ((0, 0), (0, PAD - HD)))
    bcpar = jnp.concatenate(
        [at_request(conv_state_bc).astype(F32), conv_weight_bc, conv_bias_bc[None]], axis=0
    )
    headpar = jnp.stack([dt_bias, a_log, skip_d])
    headpar = lax.dynamic_slice_in_dim(jnp.pad(headpar, ((0, 5), (0, 8))), (7 * start) // 2, 8, 1)
    state = at_request(ssm_state).reshape(-1, 64)
    state = jnp.pad(lax.dynamic_slice_in_dim(state, start * HD, HD, 0), ((0, PAD - HD), (0, 0)))
    tokens = 16 * rows
    out = pl.pallas_call(
        scan_kernel,
        in_specs=[pl.BlockSpec(memory_space=pltpu.SMEM)]
        + [pl.BlockSpec(memory_space=pltpu.VMEM)] * 5,
        out_shape=jax.ShapeDtypeStruct((tokens, PAD), BF),
        scratch_shapes=[pltpu.VMEM((tokens + 8, PAD), F32), pltpu.VMEM((tokens + 8, 128), F32)],
        compiler_params=params(),
        cost_estimate=pl.CostEstimate(
            flops=4_000_000_000, bytes_accessed=1_500_000, transcendentals=2_000_000
        ),
        name="scan",
    )(start[None], mine, par, bcpar, headpar, state)
    back = lax.all_to_all(out.reshape(16, rows, PAD), "ctx", 0, 0, tiled=True)
    return pl.pallas_call(
        unpack_kernel,
        out_shape=jax.ShapeDtypeStruct((2, rows, 8 * HD), BF),
        compiler_params=params(),
        name="unpack",
    )(back)


def gathered(value, axis):
    move = along(axis)
    half = value.shape[0] // 2
    before, after = move(value, 1), move(value, -1)
    far0, far1 = move(before[:half], 1), move(after[half:], -1)
    return after, (far0, far1), before


def sent_home(one, two, three, axis):
    move = along(axis)
    return [move(one, 1), move(three, -1), move(two, 2)]


def per_device(
    group_queries, group_keys, group_values, cache_keys, cache_values, cache_lengths, mamba_x, mamba_bc,
    mamba_dt, conv_state_x, conv_state_bc, conv_weight_x, conv_bias_x, conv_weight_bc, conv_bias_bc,
    dt_bias, a_log, skip_d, ssm_state,
):
    position = lax.axis_index("ctx")
    at_y, at_x = position // SIDE, position % SIDE
    rows = group_queries.shape[1]
    lap = jnp.arange(SIDE, dtype=jnp.int32)

    def ids(k):
        zero = ((at_y + k) % SIDE) * SIDE + (at_x + lap) % SIDE
        one = ((at_y + lap) % SIDE) * SIDE + (at_x + k) % SIDE
        return zero, one

    def info(*groups):
        pairs = [ids(k) for k in groups]
        return jnp.concatenate([position[None], *[p[0] for p in pairs], *[p[1] for p in pairs]]).astype(
            jnp.int32
        )

    first = []
    for r, axis in ((0, "x"), (1, "y")):
        own = group_queries[r]
        after, far, before = gathered(own, axis)
        first.append(jnp.concatenate([own, after, *far, before], axis=0))
    keys, values = padded_cache(
        jnp.concatenate([position[None], cache_lengths]).astype(jnp.int32),
        cache_keys, group_keys, cache_values, group_values,
    )
    near, far, back = [], [], []
    for r, axis in ((0, "y"), (1, "x")):
        a, f, b = gathered(first[r], axis)
        near.append(a), far.append(f), back.append(b)
    own0, own1 = attend(info(0), [first[0]], [first[1]], keys, values)
    side0, side1 = attend(info(1, 3), [near[0], back[0]], [near[1], back[1]], keys, values)
    far0, far1 = attend(info(2), far[0], far[1], keys, values)
    span = SIDE * rows
    total = []
    for axis, own, side, far_part in (("y", own0, side0, far0), ("x", own1, side1, far1)):
        total.append(merge([own, *sent_home(side[:span], far_part, side[span:], axis)]))
    parts = []
    for axis, value in (("x", total[0]), ("y", total[1])):
        b = [value[i * rows : (i + 1) * rows] for i in range(SIDE)]
        parts.append([b[0], *sent_home(b[1], b[2], b[3], axis)])
    attention_out = finish(*parts)
    mamba_out = state_space(
        position, mamba_x, mamba_bc, mamba_dt, conv_state_x, conv_state_bc, conv_weight_x, conv_bias_x,
        conv_weight_bc, conv_bias_bc, dt_bias, a_log, skip_d, ssm_state,
    )
    return attention_out, mamba_out


def solution(mesh):
    token = P("dp", "ctx", "head")
    placed = (
        token, token, token, token, token, P("dp"), token, P("dp", "ctx", None), token,
        P("dp", None, "head"), P("dp", None, None), P(None, "head"), P("head"), P(), P(),
        P("head"), P("head"), P("head"), P("dp", "head", None, None),
    )
    return jax.shard_map(
        per_device, mesh=mesh, in_specs=placed, out_specs=(token, token), check_vma=False
    )
```

```python
import functools
import math

import jax
import jax.numpy as jnp
from jax import lax
from jax.experimental import pallas as pl
from jax.experimental.pallas import tpu as pltpu
from jax.sharding import PartitionSpec as P

HD = 224
PAD = 256
L_LANE = 224
M_LANE = 226
NEG_FILL = -1e30
EMPTY_TOP = -8192.0
HIGHEST = lax.Precision.HIGHEST
BF = jnp.bfloat16
F32 = jnp.float32
SIDE = 4
VMEM_LIMIT = 56 * 1024 * 1024


def params(**extra):
    return pltpu.CompilerParams(vmem_limit_bytes=VMEM_LIMIT, **extra)


def shifted(value, dy, dx):
    pairs = [
        (y * SIDE + x, ((y + dy) % SIDE) * SIDE + (x + dx) % SIDE)
        for y in range(SIDE)
        for x in range(SIDE)
    ]
    return lax.ppermute(value, "ctx", pairs)


def along(axis):
    if axis == "x":
        return lambda value, step: shifted(value, 0, step)
    return lambda value, step: shifted(value, step, 0)


def widened(block, extra):
    return jnp.concatenate([block, extra], axis=1)


def pad_cache(info, request, k_ref, gk_ref, v_ref, gv_ref, ko_ref, vo_ref):
    rows = k_ref.shape[1]
    group_rows = gk_ref.shape[1]
    first = lax.axis_index("ctx") * rows
    length = info[request]
    lane = lax.broadcasted_iota(jnp.int32, (rows, PAD - HD), 1)
    row = lax.broadcasted_iota(jnp.int32, (rows, PAD - HD), 0)
    cache_bias = jnp.where((lane == 0) & (first + row >= length), NEG_FILL, 0.0).astype(BF)
    group_bias = jnp.zeros((group_rows, PAD - HD), BF)
    ones = jnp.where(lane == 0, 1.0, 0.0).astype(BF)
    for h in range(ko_ref.shape[1]):
        window = slice(h * HD, (h + 1) * HD)
        ko_ref[0, h, :rows, :] = widened(k_ref[0, :, window], cache_bias)
        ko_ref[0, h, rows:, :] = widened(gk_ref[0, :, window], group_bias)
        vo_ref[0, h, :rows, :] = widened(v_ref[0, :, window], ones)
        vo_ref[0, h, rows:, :] = widened(gv_ref[0, :, window], ones[:group_rows])


def attend_kernel(requests, groups, pads, info, *refs):
    sets = len(groups)
    count = len(requests) * sets
    q_refs, refs = refs[:count], refs[count:]
    if pads:
        raw, refs = refs[:4], refs[4:]
        outs = refs[:count]
        k_ref, v_ref, qs_ref = refs[count:]
    else:
        k_ref, v_ref = refs[:2]
        outs, qs_ref = refs[2 : 2 + count], refs[2 + count]
    turn = pl.program_id(0)
    here, rows, _ = qs_ref.shape
    block = 64
    cached = k_ref.shape[2] - block
    blocks = rows // block
    span = rows // sets
    scale = math.log2(math.e) / math.sqrt(HD)

    def on_turn(body):
        for n in range(len(requests)):
            if len(requests) == 1:
                body(n)
            else:
                pl.when(turn == n)(functools.partial(body, n))

    def fill(n):
        for at, ref in enumerate(q_refs[n * sets : (n + 1) * sets]):
            for h in range(here):
                qs_ref[h, at * span : (at + 1) * span, :] = ref[:, h * PAD : (h + 1) * PAD]

    on_turn(fill)
    if pads:
        pad_cache(info, turn, *raw, k_ref, v_ref)
    position = lax.axis_index("ctx")

    row = lax.broadcasted_iota(jnp.int32, (block, block), 0)
    col = lax.broadcasted_iota(jnp.int32, (block, block), 1) + position * block
    at_y, at_x = position // SIDE, position % SIDE
    first = turn == 0 if len(requests) == 2 else requests[0] == 0
    masks = []
    for b in range(blocks):
        along_y = jnp.where(first, groups[b // SIDE], b % SIDE)
        along_x = jnp.where(first, b % SIDE, groups[b // SIDE])
        source = ((at_y + along_y) % SIDE) * SIDE + (at_x + along_x) % SIDE
        masks.append(col <= row + source * block)
    allowed = jnp.concatenate(masks, axis=0)
    lane = lax.broadcasted_iota(jnp.int32, (rows, PAD), 1)

    def scored(i):
        return lax.dot_general(
            qs_ref[i], k_ref[0, i], (((1,), (1,)), ((), ())), preferred_element_type=F32
        )

    def summed(i, scores):
        tail = jnp.where(allowed, scores[:, cached:], NEG_FILL)
        scores = jnp.concatenate([scores[:, :cached], tail], axis=1)
        top = jnp.maximum(jnp.max(scores, axis=1, keepdims=True) * scale, EMPTY_TOP)
        top = jnp.round(top).astype(BF).astype(F32)
        weights = jnp.exp2(scores * scale - top).astype(BF)
        out = jnp.dot(weights, v_ref[0, i], preferred_element_type=F32)
        return jnp.where(lane == M_LANE, top, out).astype(BF)

    results = []
    scores = scored(0)
    for i in range(here):
        following = scored(i + 1) if i + 1 < here else None
        results.append(summed(i, scores))
        scores = following

    def store(n):
        for at in range(sets):
            for i in range(here):
                outs[n * sets + at][:, i * PAD : (i + 1) * PAD] = results[i][at * span : (at + 1) * span]

    on_turn(store)


def attend(info, requests, groups, queries, keys, values, raw=None):
    sets = len(groups)
    span, width = queries[0].shape
    rows = sets * span
    heads = width // PAD
    steps = 2
    here = heads // steps
    if raw is None:
        _, _, total, _ = keys.shape
    else:
        _, cached, _ = raw[0].shape
        group_rows = raw[1].shape[1]
        total = cached + group_rows
    base = requests[0]

    def column(n):
        def at(r, g, s):
            return 0, jnp.where(r == n, g, jnp.where(r < n, 0, steps - 1))

        return at

    kv = pl.BlockSpec((1, here, total, PAD), lambda r, g, s: (base + r, g, 0, 0))
    order = [n for n in range(len(requests)) for _ in range(sets)]
    ins = [pl.BlockSpec((span, here * PAD), column(n)) for n in order]
    outs = [pl.BlockSpec((span, here * PAD), column(n)) for n in order]
    shapes = [jax.ShapeDtypeStruct((span, heads * PAD), BF)] * len(order)
    moved = 9_000_000 * len(requests) + 6 * len(requests) * rows * width
    if raw is None:
        operands, specs = [keys, values], [kv, kv]
    else:
        operands = list(raw)
        wide = pl.BlockSpec((1, cached, here * HD), lambda r, g, s: (r, 0, g))
        small = pl.BlockSpec((1, group_rows, here * HD), lambda r, g, s: (r, 0, g))
        specs = [wide, small, wide, small]
        outs += [kv, kv]
        shapes += [jax.ShapeDtypeStruct((len(requests), heads, total, PAD), BF)] * 2
        moved += 16_000_000
    work = len(requests) * heads * rows * total
    return pl.pallas_call(
        functools.partial(attend_kernel, requests, groups, raw is not None),
        grid_spec=pltpu.PrefetchScalarGridSpec(
            num_scalar_prefetch=1,
            grid=(len(requests), steps),
            in_specs=[*ins, *specs],
            out_specs=outs,
            scratch_shapes=[pltpu.VMEM((here, rows, PAD), BF)],
        ),
        out_shape=shapes,
        compiler_params=params(),
        cost_estimate=pl.CostEstimate(flops=6 * work * PAD, bytes_accessed=moved, transcendentals=work),
        name="attend",
    )(info, *queries, *operands)


def join_kernel(own_ref, *refs):
    outs = refs[6:]
    rows = own_ref.shape[1]
    lane = lax.broadcasted_iota(jnp.int32, (rows, PAD - HD), 1)
    ones = jnp.where(lane == 0, 1.0, 0.0).astype(BF)
    for r, out in enumerate(outs):
        blocks = [own_ref.at[r], *refs[3 * r : 3 * r + 3]]
        for n, ref in enumerate(blocks):
            for h in range(own_ref.shape[2] // HD):
                out[n * rows : (n + 1) * rows, h * PAD : (h + 1) * PAD] = widened(
                    ref[:, h * HD : (h + 1) * HD], ones
                )


def joined_rows(own, others0, others1):
    _, rows, width = own.shape
    padded = width // HD * PAD
    return pl.pallas_call(
        join_kernel,
        out_shape=[jax.ShapeDtypeStruct((SIDE * rows, padded), BF)] * 2,
        compiler_params=params(),
        cost_estimate=pl.CostEstimate(flops=0, bytes_accessed=16 * rows * width * 2, transcendentals=0),
        name="join",
    )(own, *others0, *others1)


def merged(parts):
    tops = [part[:, M_LANE : M_LANE + 1] for part in parts]
    top = functools.reduce(jnp.maximum, tops)
    return sum(part * jnp.exp2(own - top) for part, own in zip(parts, tops)), top


def merge_kernel(*refs):
    parts, outs = refs[:4], refs[4:]
    rows = outs[0].shape[0]
    lane = lax.broadcasted_iota(jnp.int32, (rows, PAD), 1)
    for h in range(outs[0].shape[1] // PAD):
        window = slice(h * PAD, (h + 1) * PAD)
        for b in range(SIDE):
            at = slice(b * rows, (b + 1) * rows)
            total, top = merged([ref[at, window].astype(F32) for ref in parts])
            outs[b][:, window] = jnp.where(lane == M_LANE, top, total).astype(BF)


def merge(parts):
    rows, width = parts[0].shape
    steps = 2
    spec = pl.BlockSpec((rows, width // steps), lambda i: (0, i))
    out = pl.BlockSpec((rows // SIDE, width // steps), lambda i: (0, i))
    return pl.pallas_call(
        merge_kernel,
        grid=(steps,),
        in_specs=[spec] * 4,
        out_specs=[out] * 4,
        out_shape=[jax.ShapeDtypeStruct((rows // SIDE, width), BF)] * 4,
        compiler_params=params(),
        cost_estimate=pl.CostEstimate(
            flops=rows * width * 8, bytes_accessed=rows * width * 10, transcendentals=0
        ),
        name="merge",
    )(*parts)


def finish_kernel(count, *refs):
    out_ref = refs[2 * count]
    heads = out_ref.shape[2] // HD
    for r in range(2):
        done = []
        for h in range(heads):
            window = slice(h * PAD, (h + 1) * PAD)
            total, _ = merged([ref[:, window].astype(F32) for ref in refs[r * count : (r + 1) * count]])
            done.append((total / total[:, L_LANE : L_LANE + 1])[:, :HD])
        out_ref[r] = jnp.concatenate(done, axis=1).astype(BF)


def finish(parts0, parts1):
    rows, width = parts0[0].shape
    heads = width // PAD
    return pl.pallas_call(
        functools.partial(finish_kernel, len(parts0)),
        out_shape=jax.ShapeDtypeStruct((2, rows, heads * HD), BF),
        compiler_params=params(),
        cost_estimate=pl.CostEstimate(
            flops=rows * width * 16, bytes_accessed=rows * width * 20, transcendentals=0
        ),
        name="finish",
    )(*parts0, *parts1)


def pack_kernel(x_ref, dt_ref, bc_ref, out_ref):
    rows = x_ref.shape[1]
    heads = dt_ref.shape[2]
    for r in range(2):
        extra = jnp.concatenate([dt_ref[r], jnp.zeros((rows, PAD - HD - heads), BF)], axis=1)
        for c in range(8):
            out_ref[r * 8 + c, :, :PAD] = jnp.concatenate(
                [x_ref[r, :, c * HD : (c + 1) * HD], extra], axis=1
            )
            out_ref[r * 8 + c, :, PAD:] = bc_ref[r]


def unpack_kernel(in_ref, out_ref):
    for r in range(2):
        out_ref[r] = jnp.concatenate(
            [in_ref[r * 8 + c].astype(F32)[:, :HD] for c in range(8)], axis=1
        ).astype(BF)


def split(value):
    high = value.astype(BF)
    return high, (value - high.astype(F32)).astype(BF)


def split_three(value):
    high = value.astype(BF)
    rest = value - high.astype(F32)
    middle, low = split(rest)
    return high, middle, low


def scan_kernel(
    info, data_ref, cx_ref, wx_ref, bx_ref, cb_ref, wb_ref, bb_ref, head_ref, state_ref, out_ref,
    xs_ref, bcs_ref, par_ref,
):
    tokens = data_ref.shape[0]
    chunk = 128
    request, start = info[0], info[1]
    first_head = (7 * start) // 2
    taps = wx_ref.shape[0]
    rim = taps - 1
    before = 8 - rim
    for c in range(8):

        @pl.when(start == c)
        def _():
            window = slice(c * HD, (c + 1) * HD)
            par_ref[0:taps, :HD] = wx_ref[:, window]
            par_ref[taps : taps + 1, :HD] = bx_ref[:, window]
            xs_ref[before:8, :HD] = cx_ref[request].astype(F32)[:, window]

    par_ref[:, HD:] = jnp.zeros((8, PAD - HD), F32)
    xs_ref[0:8, HD:] = jnp.zeros((8, PAD - HD), F32)
    bcs_ref[before:8, :] = cb_ref[request].astype(F32)
    xs_ref[8:, :] = data_ref[:, :PAD].astype(F32)
    bcs_ref[8:, :] = data_ref[:, PAD:].astype(F32)

    lane = lax.broadcasted_iota(jnp.int32, (8, PAD), 1) + start * HD
    head = lax.broadcasted_iota(jnp.int32, (8, PAD), 0) + first_head
    spread = (lane // 64 == head).astype(F32)
    spread3 = jnp.concatenate([spread] * 3, axis=0).astype(BF)
    pick = (
        lax.broadcasted_iota(jnp.int32, (128, 8), 0)
        == lax.broadcasted_iota(jnp.int32, (128, 8), 1) + (HD - 128) + first_head
    ).astype(F32)
    headpar = jnp.dot(head_ref[...], pick, precision=HIGHEST, preferred_element_type=F32)
    dt_bias, rate, skip = headpar[0:1], jnp.exp(headpar[1:2]), headpar[2:3]
    skip_wide = jnp.dot(skip, spread, precision=HIGHEST, preferred_element_type=F32)
    row = lax.broadcasted_iota(jnp.int32, (chunk, chunk), 0)
    col = lax.broadcasted_iota(jnp.int32, (chunk, chunk), 1)
    lower = row >= col
    lower_b = lower.astype(F32).astype(BF)
    pick_b = pick.astype(BF)
    masks = [spread[h : h + 1] for h in range(4)]
    state = jnp.concatenate(
        [state_ref[0, pl.ds(pl.multiple_of(start * HD, 32), HD), :], jnp.zeros((PAD - HD, 64), F32)], axis=0
    ).T
    for c in range(tokens // chunk):
        at = c * chunk
        x = jnp.zeros((chunk, PAD), F32) + par_ref[taps : taps + 1, :]
        bc = jnp.zeros((chunk, 128), F32) + bb_ref[...]
        for i in range(taps):
            x = x + par_ref[i : i + 1, :] * xs_ref[at + before + i : at + before + i + chunk, :]
            bc = bc + wb_ref[i : i + 1, :] * bcs_ref[at + before + i : at + before + i + chunk, :]
        x = x * jax.nn.sigmoid(x)
        bc = bc * jax.nn.sigmoid(bc)
        b, o = bc[:, :64], bc[:, 64:]
        raw = data_ref[at : at + chunk, 128:PAD]
        size = jnp.dot(raw, pick_b, preferred_element_type=F32) + dt_bias
        size = jnp.maximum(size, 0.0) + jnp.log1p(jnp.exp(-jnp.abs(size)))
        run = jnp.dot(
            lower_b, jnp.concatenate(split_three(-rate * size), axis=1), preferred_element_type=F32
        )
        run = run[:, :8] + run[:, 8:16] + run[:, 16:24]
        run_t = run.T
        wide = jnp.dot(
            jnp.concatenate(split_three(jnp.concatenate([size, run], axis=0)), axis=1),
            spread3,
            preferred_element_type=F32,
        )
        size_wide, run_wide = wide[:chunk], wide[chunk:]
        xdt = x * size_wide
        o_high, o_low = split(o)
        b_high, b_low = split(b)
        o_three = jnp.concatenate([o_high, o_high, o_low], axis=1)
        cross = lax.dot_general(
            o_three,
            jnp.concatenate([b_high, b_low, b_high], axis=1),
            (((1,), (1,)), ((), ())),
            preferred_element_type=F32,
        )
        pieces, mixes = [], []
        for h in range(4):
            gap = run[:, h : h + 1] - run_t[h : h + 1, :]
            mixes.append((jnp.exp(jnp.where(lower, gap, NEG_FILL)) * cross).astype(BF))
            pieces.append((xdt * masks[h]).astype(BF))
        y = jnp.dot(
            jnp.concatenate(mixes, axis=1), jnp.concatenate(pieces, axis=0), preferred_element_type=F32
        )
        s_high, s_low = split(state)
        y = y + jnp.exp(run_wide) * jnp.dot(
            o_three, jnp.concatenate([s_high, s_low, s_high], axis=0), preferred_element_type=F32
        )
        last = run_wide[chunk - 1 : chunk]
        w_high, w_low = split(xdt * jnp.exp(last - run_wide))
        state = state * jnp.exp(last) + lax.dot_general(
            jnp.concatenate([b_high, b_high, b_low], axis=0),
            jnp.concatenate([w_high, w_low, w_high], axis=0),
            (((0,), (0,)), ((), ())),
            preferred_element_type=F32,
        )
        out_ref[at : at + chunk, :] = (y + skip_wide * x).astype(BF)


def channels_in(mamba_x, mamba_bc, mamba_dt):
    rows = mamba_x.shape[1]
    packed = pl.pallas_call(
        pack_kernel,
        out_shape=jax.ShapeDtypeStruct((16, rows, PAD + 128), BF),
        compiler_params=params(),
        name="pack",
    )(mamba_x, mamba_dt, mamba_bc)
    return packed, lax.all_to_all(packed, "ctx", 0, 0, tiled=True).reshape(16 * rows, PAD + 128)


def state_space(
    position, mine, conv_state_x, conv_state_bc, conv_weight_x, conv_bias_x, conv_weight_bc,
    conv_bias_bc, dt_bias, a_log, skip_d, ssm_state,
):
    rows = mine.shape[0] // 16
    heads = dt_bias.shape[0]
    headpar = jnp.pad(jnp.stack([dt_bias, a_log, skip_d]), ((0, 5), (HD - 128, 128 - (HD - 128) - heads)))
    state = ssm_state.reshape(2, -1, 64)
    tokens = 16 * rows

    def whole(value):
        return pl.BlockSpec(value.shape, lambda i, s: (0,) * value.ndim)

    operands = (
        mine, conv_state_x, conv_weight_x, conv_bias_x[None], conv_state_bc, conv_weight_bc,
        conv_bias_bc[None], headpar,
    )
    out = pl.pallas_call(
        scan_kernel,
        grid_spec=pltpu.PrefetchScalarGridSpec(
            num_scalar_prefetch=1,
            grid=(1,),
            in_specs=[*map(whole, operands), pl.BlockSpec((1, *state.shape[1:]), lambda i, s: (s[0], 0, 0))],
            out_specs=pl.BlockSpec((tokens, PAD), lambda i, s: (0, 0)),
            scratch_shapes=[
                pltpu.VMEM((tokens + 8, PAD), F32),
                pltpu.VMEM((tokens + 8, 128), F32),
                pltpu.VMEM((8, PAD), F32),
            ],
        ),
        out_shape=jax.ShapeDtypeStruct((tokens, PAD), BF),
        compiler_params=params(),
        cost_estimate=pl.CostEstimate(
            flops=8_000_000_000, bytes_accessed=2_500_000, transcendentals=2_000_000
        ),
        name="scan",
    )(jnp.stack([position // 8, position % 8]).astype(jnp.int32), *operands, state)
    return out.reshape(16, rows, PAD)


def unpacked(back):
    return pl.pallas_call(
        unpack_kernel,
        out_shape=jax.ShapeDtypeStruct((2, back.shape[1], 8 * HD), BF),
        compiler_params=params(),
        name="unpack",
    )(back)


def after(values, done):
    return lax.optimization_barrier((values, done))[0]


def sent_home(one, two, three, axis):
    move = along(axis)
    return [move(one, 1), move(three, -1), move(two, 2)]


def per_device(
    group_queries, group_keys, group_values, cache_keys, cache_values, cache_lengths, mamba_x, mamba_bc,
    mamba_dt, conv_state_x, conv_state_bc, conv_weight_x, conv_bias_x, conv_weight_bc, conv_bias_bc,
    dt_bias, a_log, skip_d, ssm_state,
):
    position = lax.axis_index("ctx")
    info = cache_lengths
    queries = [group_queries[0], group_queries[1]]
    moves = [along("x"), along("y")]
    others = [[move(q, -1), move(q, 2), move(q, 1)] for q, move in zip(queries, moves)]
    packed, mine = channels_in(after(mamba_x, others[0][0]), mamba_bc, mamba_dt)
    first0, first1 = joined_rows(after(group_queries, packed), *others)
    far0, far1 = moves[1](first0, 2), moves[0](first1, 2)
    own0, own1, keys, values = attend(
        info, (0, 1), (0,), [first0, first1], None, None,
        (cache_keys, group_keys, cache_values, group_values),
    )
    first0, first1 = after((first0, first1), (far0, far1))
    after0, before0 = moves[1](first0, -1), moves[1](first0, 1)
    after1, before1 = moves[0](first1, -1), moves[0](first1, 1)
    two0, two1 = attend(after(info, own0), (0, 1), (2,), [far0, far1], keys, values)
    two0, two1 = after((two0, two1), (after0, before0, after1, before1))
    one0, three0, one1, three1 = attend(
        after(info, (two0, mine)), (0, 1), (1, 3), [after0, before0, after1, before1], keys, values
    )
    two0, two1 = moves[1](two0, 2), moves[0](two1, 2)
    scan_inputs = (
        mine, conv_state_x, conv_state_bc, conv_weight_x, conv_bias_x, conv_weight_bc, conv_bias_bc,
        dt_bias, a_log, skip_d, ssm_state,
    )
    scanned = state_space(position, *after(scan_inputs, one0))
    back = lax.all_to_all(scanned, "ctx", 0, 0, tiled=True)
    one0, three0, one1, three1 = after((one0, three0, one1, three1), (two0, two1))
    side0 = [moves[1](one0, 1), moves[1](three0, -1)]
    side1 = [moves[0](one1, 1), moves[0](three1, -1)]
    blocks0 = merge([after(own0, scanned), *side0, two0])
    home0 = [blocks0[0], *sent_home(*blocks0[1:], "x")]
    blocks1 = merge([after(own1, blocks0[0]), *side1, two1])
    home1 = [blocks1[0], *sent_home(*blocks1[1:], "y")]
    return finish(home0, home1), unpacked(back)


def solution(mesh):
    token = P("dp", "ctx", "head")
    placed = (
        token, token, token, token, token, P("dp"), token, P("dp", "ctx", None), token,
        P("dp", None, "head"), P("dp", None, None), P(None, "head"), P("head"), P(), P(),
        P("head"), P("head"), P("head"), P("dp", "head", None, None),
    )
    return jax.shard_map(
        per_device, mesh=mesh, in_specs=placed, out_specs=(token, token), check_vma=False
    )
```

```python
import functools
import math

import jax
import jax.numpy as jnp
from jax import lax
from jax.experimental import pallas as pl
from jax.experimental.pallas import tpu as pltpu
from jax.sharding import PartitionSpec as P

HD = 224
PAD = 256
L_LANE = 224
M_LANE = 226
NEG_FILL = -1e30
EMPTY_TOP = -8192.0
HIGHEST = lax.Precision.HIGHEST
BF = jnp.bfloat16
F32 = jnp.float32
SIDE = 4
VMEM_LIMIT = 56 * 1024 * 1024


def params(**extra):
    return pltpu.CompilerParams(vmem_limit_bytes=VMEM_LIMIT, **extra)


def shifted(value, dy, dx):
    pairs = [
        (y * SIDE + x, ((y + dy) % SIDE) * SIDE + (x + dx) % SIDE)
        for y in range(SIDE)
        for x in range(SIDE)
    ]
    return lax.ppermute(value, "ctx", pairs)


def along(axis):
    if axis == "x":
        return lambda value, step: shifted(value, 0, step)
    return lambda value, step: shifted(value, step, 0)


def widened(block, extra):
    return jnp.concatenate([block, extra], axis=1)


def pad_cache(info, request, k_ref, gk_ref, v_ref, gv_ref, ko_ref, vo_ref):
    rows = k_ref.shape[1]
    group_rows = gk_ref.shape[1]
    first = lax.axis_index("ctx") * rows
    length = info[request]
    lane = lax.broadcasted_iota(jnp.int32, (rows, PAD - HD), 1)
    row = lax.broadcasted_iota(jnp.int32, (rows, PAD - HD), 0)
    cache_bias = jnp.where((lane == 0) & (first + row >= length), NEG_FILL, 0.0).astype(BF)
    group_bias = jnp.zeros((group_rows, PAD - HD), BF)
    ones = jnp.where(lane == 0, 1.0, 0.0).astype(BF)
    for h in range(ko_ref.shape[1]):
        window = slice(h * HD, (h + 1) * HD)
        ko_ref[0, h, :rows, :] = widened(k_ref[0, :, window], cache_bias)
        ko_ref[0, h, rows:, :] = widened(gk_ref[0, :, window], group_bias)
        vo_ref[0, h, :rows, :] = widened(v_ref[0, :, window], ones)
        vo_ref[0, h, rows:, :] = widened(gv_ref[0, :, window], ones[:group_rows])


def attend_kernel(requests, groups, pads, info, *refs):
    sets = len(groups)
    count = len(requests) * sets
    q_refs, refs = refs[:count], refs[count:]
    if pads:
        raw, refs = refs[:4], refs[4:]
        outs, (k_ref, v_ref) = refs[:count], refs[count:]
    else:
        (k_ref, v_ref), outs = refs[:2], refs[2:]
    turn = pl.program_id(0)
    here = k_ref.shape[1]
    span = q_refs[0].shape[0]
    rows = sets * span
    block = 64
    cached = k_ref.shape[2] - block
    scale = math.log2(math.e) / math.sqrt(HD)
    if pads:
        pad_cache(info, turn, *raw, k_ref, v_ref)
    position = lax.axis_index("ctx")

    def body(n):
        row = lax.broadcasted_iota(jnp.int32, (block, block), 0)
        col = lax.broadcasted_iota(jnp.int32, (block, block), 1) + position * block
        masks = []
        for group in groups:
            for lap in range(SIDE):
                along_y, along_x = (group, lap) if requests[n] == 0 else (lap, group)
                source = ((position // SIDE + along_y) % SIDE) * SIDE + (position % SIDE + along_x) % SIDE
                masks.append(col <= row + source * block)
        allowed = jnp.concatenate(masks, axis=0)
        lane = lax.broadcasted_iota(jnp.int32, (rows, PAD), 1)
        mine = q_refs[n * sets : (n + 1) * sets]

        def scored(i):
            queries = [ref[:, i * PAD : (i + 1) * PAD] for ref in mine]
            return lax.dot_general(
                jnp.concatenate(queries, axis=0) if sets > 1 else queries[0],
                k_ref[0, i],
                (((1,), (1,)), ((), ())),
                preferred_element_type=F32,
            )

        def store(i, scores):
            tail = jnp.where(allowed, scores[:, cached:], NEG_FILL)
            scores = jnp.concatenate([scores[:, :cached], tail], axis=1)
            top = jnp.maximum(jnp.max(scores, axis=1, keepdims=True) * scale, EMPTY_TOP)
            top = jnp.round(top).astype(BF).astype(F32)
            weights = jnp.exp2(scores * scale - top).astype(BF)
            out = jnp.dot(weights, v_ref[0, i], preferred_element_type=F32)
            out = jnp.where(lane == M_LANE, top, out).astype(BF)
            for at in range(sets):
                outs[n * sets + at][:, i * PAD : (i + 1) * PAD] = out[at * span : (at + 1) * span]

        scores = scored(0)
        for i in range(here):
            following = scored(i + 1) if i + 1 < here else None
            store(i, scores)
            scores = following

    for n in range(len(requests)):
        if len(requests) == 1:
            body(n)
        else:
            pl.when(turn == n)(functools.partial(body, n))


def attend(info, requests, groups, queries, keys, values, raw=None):
    sets = len(groups)
    span, width = queries[0].shape
    rows = sets * span
    heads = width // PAD
    steps = 2
    here = heads // steps
    if raw is None:
        _, _, total, _ = keys.shape
    else:
        _, cached, _ = raw[0].shape
        group_rows = raw[1].shape[1]
        total = cached + group_rows
    base = requests[0]

    def column(n):
        def at(r, g, s):
            return 0, jnp.where(r == n, g, jnp.where(r < n, 0, steps - 1))

        return at

    kv = pl.BlockSpec((1, here, total, PAD), lambda r, g, s: (base + r, g, 0, 0))
    order = [n for n in range(len(requests)) for _ in range(sets)]
    ins = [pl.BlockSpec((span, here * PAD), column(n)) for n in order]
    outs = [pl.BlockSpec((span, here * PAD), column(n)) for n in order]
    shapes = [jax.ShapeDtypeStruct((span, heads * PAD), BF)] * len(order)
    moved = 9_000_000 * len(requests) + 6 * len(requests) * rows * width
    if raw is None:
        operands, specs = [keys, values], [kv, kv]
    else:
        operands = list(raw)
        wide = pl.BlockSpec((1, cached, here * HD), lambda r, g, s: (r, 0, g))
        small = pl.BlockSpec((1, group_rows, here * HD), lambda r, g, s: (r, 0, g))
        specs = [wide, small, wide, small]
        outs += [kv, kv]
        shapes += [jax.ShapeDtypeStruct((len(requests), heads, total, PAD), BF)] * 2
        moved += 16_000_000
    work = len(requests) * heads * rows * total
    return pl.pallas_call(
        functools.partial(attend_kernel, requests, groups, raw is not None),
        grid_spec=pltpu.PrefetchScalarGridSpec(
            num_scalar_prefetch=1,
            grid=(len(requests), steps),
            in_specs=[*ins, *specs],
            out_specs=outs,
        ),
        out_shape=shapes,
        compiler_params=params(),
        cost_estimate=pl.CostEstimate(flops=6 * work * PAD, bytes_accessed=moved, transcendentals=work),
        name="attend",
    )(info, *queries, *operands)


def join_kernel(own_ref, *refs):
    outs = refs[6:]
    rows = own_ref.shape[1]
    lane = lax.broadcasted_iota(jnp.int32, (rows, PAD - HD), 1)
    ones = jnp.where(lane == 0, 1.0, 0.0).astype(BF)
    for r, out in enumerate(outs):
        blocks = [own_ref.at[r], *refs[3 * r : 3 * r + 3]]
        for n, ref in enumerate(blocks):
            for h in range(own_ref.shape[2] // HD):
                out[n * rows : (n + 1) * rows, h * PAD : (h + 1) * PAD] = widened(
                    ref[:, h * HD : (h + 1) * HD], ones
                )


def joined_rows(own, others0, others1):
    _, rows, width = own.shape
    padded = width // HD * PAD
    return pl.pallas_call(
        join_kernel,
        out_shape=[jax.ShapeDtypeStruct((SIDE * rows, padded), BF)] * 2,
        compiler_params=params(),
        cost_estimate=pl.CostEstimate(flops=0, bytes_accessed=16 * rows * width * 2, transcendentals=0),
        name="join",
    )(own, *others0, *others1)


def merged(parts):
    tops = [part[:, M_LANE : M_LANE + 1] for part in parts]
    top = functools.reduce(jnp.maximum, tops)
    return sum(part * jnp.exp2(own - top) for part, own in zip(parts, tops)), top


def merge_kernel(*refs):
    parts, outs = refs[:4], refs[4:]
    rows = outs[0].shape[0]
    lane = lax.broadcasted_iota(jnp.int32, (rows, PAD), 1)
    for h in range(outs[0].shape[1] // PAD):
        window = slice(h * PAD, (h + 1) * PAD)
        for b in range(SIDE):
            at = slice(b * rows, (b + 1) * rows)
            total, top = merged([ref[at, window].astype(F32) for ref in parts])
            outs[b][:, window] = jnp.where(lane == M_LANE, top, total).astype(BF)


def merge(parts):
    rows, width = parts[0].shape
    steps = 2
    spec = pl.BlockSpec((rows, width // steps), lambda i: (0, i))
    out = pl.BlockSpec((rows // SIDE, width // steps), lambda i: (0, i))
    return pl.pallas_call(
        merge_kernel,
        grid=(steps,),
        in_specs=[spec] * 4,
        out_specs=[out] * 4,
        out_shape=[jax.ShapeDtypeStruct((rows // SIDE, width), BF)] * 4,
        compiler_params=params(),
        cost_estimate=pl.CostEstimate(
            flops=rows * width * 8, bytes_accessed=rows * width * 10, transcendentals=0
        ),
        name="merge",
    )(*parts)


def finish_kernel(count, *refs):
    out_ref = refs[2 * count]
    heads = out_ref.shape[2] // HD
    for r in range(2):
        done = []
        for h in range(heads):
            window = slice(h * PAD, (h + 1) * PAD)
            total, _ = merged([ref[:, window].astype(F32) for ref in refs[r * count : (r + 1) * count]])
            done.append((total / total[:, L_LANE : L_LANE + 1])[:, :HD])
        out_ref[r] = jnp.concatenate(done, axis=1).astype(BF)


def finish(parts0, parts1):
    rows, width = parts0[0].shape
    heads = width // PAD
    return pl.pallas_call(
        functools.partial(finish_kernel, len(parts0)),
        out_shape=jax.ShapeDtypeStruct((2, rows, heads * HD), BF),
        compiler_params=params(),
        cost_estimate=pl.CostEstimate(
            flops=rows * width * 16, bytes_accessed=rows * width * 20, transcendentals=0
        ),
        name="finish",
    )(*parts0, *parts1)


def pack_kernel(x_ref, dt_ref, bc_ref, out_ref):
    rows = x_ref.shape[1]
    heads = dt_ref.shape[2]
    for r in range(2):
        extra = jnp.concatenate([dt_ref[r], jnp.zeros((rows, PAD - HD - heads), BF)], axis=1)
        for c in range(8):
            out_ref[r * 8 + c, :, :PAD] = jnp.concatenate(
                [x_ref[r, :, c * HD : (c + 1) * HD], extra], axis=1
            )
            out_ref[r * 8 + c, :, PAD:] = bc_ref[r]


def unpack_kernel(in_ref, out_ref):
    for r in range(2):
        out_ref[r] = jnp.concatenate(
            [in_ref[r * 8 + c].astype(F32)[:, :HD] for c in range(8)], axis=1
        ).astype(BF)


def split(value):
    high = value.astype(BF)
    return high, (value - high.astype(F32)).astype(BF)


def split_three(value):
    high = value.astype(BF)
    rest = value - high.astype(F32)
    middle, low = split(rest)
    return high, middle, low


def scan_kernel(
    info, data_ref, cx_ref, wx_ref, bx_ref, cb_ref, wb_ref, bb_ref, head_ref, state_ref, out_ref,
    xs_ref, bcs_ref, par_ref,
):
    tokens = data_ref.shape[0]
    chunk = 128
    request, start = info[0], info[1]
    first_head = (7 * start) // 2
    taps = wx_ref.shape[0]
    rim = taps - 1
    before = 8 - rim
    for c in range(8):

        @pl.when(start == c)
        def _():
            window = slice(c * HD, (c + 1) * HD)
            par_ref[0:taps, :HD] = wx_ref[:, window]
            par_ref[taps : taps + 1, :HD] = bx_ref[:, window]
            xs_ref[before:8, :HD] = cx_ref[request].astype(F32)[:, window]

    par_ref[:, HD:] = jnp.zeros((8, PAD - HD), F32)
    xs_ref[0:8, HD:] = jnp.zeros((8, PAD - HD), F32)
    bcs_ref[before:8, :] = cb_ref[request].astype(F32)
    xs_ref[8:, :] = data_ref[:, :PAD].astype(F32)
    bcs_ref[8:, :] = data_ref[:, PAD:].astype(F32)

    lane = lax.broadcasted_iota(jnp.int32, (8, PAD), 1) + start * HD
    head = lax.broadcasted_iota(jnp.int32, (8, PAD), 0) + first_head
    spread = (lane // 64 == head).astype(F32)
    spread3 = jnp.concatenate([spread] * 3, axis=0).astype(BF)
    pick = (
        lax.broadcasted_iota(jnp.int32, (128, 8), 0)
        == lax.broadcasted_iota(jnp.int32, (128, 8), 1) + (HD - 128) + first_head
    ).astype(F32)
    headpar = jnp.dot(head_ref[...], pick, precision=HIGHEST, preferred_element_type=F32)
    dt_bias, rate, skip = headpar[0:1], jnp.exp(headpar[1:2]), headpar[2:3]
    skip_wide = jnp.dot(skip, spread, precision=HIGHEST, preferred_element_type=F32)
    row = lax.broadcasted_iota(jnp.int32, (chunk, chunk), 0)
    col = lax.broadcasted_iota(jnp.int32, (chunk, chunk), 1)
    lower = row >= col
    lower_b = lower.astype(F32).astype(BF)
    pick_b = pick.astype(BF)
    masks = [spread[h : h + 1] for h in range(4)]
    state = jnp.concatenate(
        [state_ref[0, pl.ds(pl.multiple_of(start * HD, 32), HD), :], jnp.zeros((PAD - HD, 64), F32)], axis=0
    ).T
    for c in range(tokens // chunk):
        at = c * chunk
        x = jnp.zeros((chunk, PAD), F32) + par_ref[taps : taps + 1, :]
        bc = jnp.zeros((chunk, 128), F32) + bb_ref[...]
        for i in range(taps):
            x = x + par_ref[i : i + 1, :] * xs_ref[at + before + i : at + before + i + chunk, :]
            bc = bc + wb_ref[i : i + 1, :] * bcs_ref[at + before + i : at + before + i + chunk, :]
        x = x * jax.nn.sigmoid(x)
        bc = bc * jax.nn.sigmoid(bc)
        b, o = bc[:, :64], bc[:, 64:]
        raw = data_ref[at : at + chunk, 128:PAD]
        size = jnp.dot(raw, pick_b, preferred_element_type=F32) + dt_bias
        size = jnp.maximum(size, 0.0) + jnp.log1p(jnp.exp(-jnp.abs(size)))
        run = jnp.dot(
            lower_b, jnp.concatenate(split_three(-rate * size), axis=1), preferred_element_type=F32
        )
        run = run[:, :8] + run[:, 8:16] + run[:, 16:24]
        run_t = run.T
        wide = jnp.dot(
            jnp.concatenate(split_three(jnp.concatenate([size, run], axis=0)), axis=1),
            spread3,
            preferred_element_type=F32,
        )
        size_wide, run_wide = wide[:chunk], wide[chunk:]
        xdt = x * size_wide
        o_high, o_low = split(o)
        b_high, b_low = split(b)
        o_three = jnp.concatenate([o_high, o_high, o_low], axis=1)
        cross = lax.dot_general(
            o_three,
            jnp.concatenate([b_high, b_low, b_high], axis=1),
            (((1,), (1,)), ((), ())),
            preferred_element_type=F32,
        )
        pieces, mixes = [], []
        for h in range(4):
            gap = run[:, h : h + 1] - run_t[h : h + 1, :]
            mixes.append((jnp.exp(jnp.where(lower, gap, NEG_FILL)) * cross).astype(BF))
            pieces.append((xdt * masks[h]).astype(BF))
        y = jnp.dot(
            jnp.concatenate(mixes, axis=1), jnp.concatenate(pieces, axis=0), preferred_element_type=F32
        )
        s_high, s_low = split(state)
        y = y + jnp.exp(run_wide) * jnp.dot(
            o_three, jnp.concatenate([s_high, s_low, s_high], axis=0), preferred_element_type=F32
        )
        last = run_wide[chunk - 1 : chunk]
        w_high, w_low = split(xdt * jnp.exp(last - run_wide))
        state = state * jnp.exp(last) + lax.dot_general(
            jnp.concatenate([b_high, b_high, b_low], axis=0),
            jnp.concatenate([w_high, w_low, w_high], axis=0),
            (((0,), (0,)), ((), ())),
            preferred_element_type=F32,
        )
        out_ref[at : at + chunk, :] = (y + skip_wide * x).astype(BF)


def channels_in(mamba_x, mamba_bc, mamba_dt):
    rows = mamba_x.shape[1]
    packed = pl.pallas_call(
        pack_kernel,
        out_shape=jax.ShapeDtypeStruct((16, rows, PAD + 128), BF),
        compiler_params=params(),
        name="pack",
    )(mamba_x, mamba_dt, mamba_bc)
    return packed, lax.all_to_all(packed, "ctx", 0, 0, tiled=True).reshape(16 * rows, PAD + 128)


def state_space(
    position, mine, conv_state_x, conv_state_bc, conv_weight_x, conv_bias_x, conv_weight_bc,
    conv_bias_bc, dt_bias, a_log, skip_d, ssm_state,
):
    rows = mine.shape[0] // 16
    heads = dt_bias.shape[0]
    headpar = jnp.pad(jnp.stack([dt_bias, a_log, skip_d]), ((0, 5), (HD - 128, 128 - (HD - 128) - heads)))
    state = ssm_state.reshape(2, -1, 64)
    tokens = 16 * rows

    def whole(value):
        return pl.BlockSpec(value.shape, lambda i, s: (0,) * value.ndim)

    operands = (
        mine, conv_state_x, conv_weight_x, conv_bias_x[None], conv_state_bc, conv_weight_bc,
        conv_bias_bc[None], headpar,
    )
    out = pl.pallas_call(
        scan_kernel,
        grid_spec=pltpu.PrefetchScalarGridSpec(
            num_scalar_prefetch=1,
            grid=(1,),
            in_specs=[*map(whole, operands), pl.BlockSpec((1, *state.shape[1:]), lambda i, s: (s[0], 0, 0))],
            out_specs=pl.BlockSpec((tokens, PAD), lambda i, s: (0, 0)),
            scratch_shapes=[
                pltpu.VMEM((tokens + 8, PAD), F32),
                pltpu.VMEM((tokens + 8, 128), F32),
                pltpu.VMEM((8, PAD), F32),
            ],
        ),
        out_shape=jax.ShapeDtypeStruct((tokens, PAD), BF),
        compiler_params=params(),
        cost_estimate=pl.CostEstimate(
            flops=8_000_000_000, bytes_accessed=2_500_000, transcendentals=2_000_000
        ),
        name="scan",
    )(jnp.stack([position // 8, position % 8]).astype(jnp.int32), *operands, state)
    return out.reshape(16, rows, PAD)


def unpacked(back):
    return pl.pallas_call(
        unpack_kernel,
        out_shape=jax.ShapeDtypeStruct((2, back.shape[1], 8 * HD), BF),
        compiler_params=params(),
        name="unpack",
    )(back)


def after(values, done):
    return lax.optimization_barrier((values, done))[0]


def sent_home(one, two, three, axis):
    move = along(axis)
    return [move(one, 1), move(three, -1), move(two, 2)]


def per_device(
    group_queries, group_keys, group_values, cache_keys, cache_values, cache_lengths, mamba_x, mamba_bc,
    mamba_dt, conv_state_x, conv_state_bc, conv_weight_x, conv_bias_x, conv_weight_bc, conv_bias_bc,
    dt_bias, a_log, skip_d, ssm_state,
):
    position = lax.axis_index("ctx")
    info = cache_lengths
    queries = [group_queries[0], group_queries[1]]
    moves = [along("x"), along("y")]
    others = [[move(q, -1), move(q, 2), move(q, 1)] for q, move in zip(queries, moves)]
    packed, mine = channels_in(after(mamba_x, others[0][0]), mamba_bc, mamba_dt)
    first0, first1 = joined_rows(after(group_queries, packed), *others)
    far0, far1 = moves[1](first0, 2), moves[0](first1, 2)
    own0, own1, keys, values = attend(
        info, (0, 1), (0,), [first0, first1], None, None,
        (cache_keys, group_keys, cache_values, group_values),
    )
    first0, first1 = after((first0, first1), (far0, far1, own0))
    after0, before0 = moves[1](first0, -1), moves[1](first0, 1)
    after1, before1 = moves[0](first1, -1), moves[0](first1, 1)
    two0, two1 = attend(after(info, (own0, mine)), (0, 1), (2,), [far0, far1], keys, values)
    two0, two1 = after((two0, two1), (after0, before0, after1, before1))
    one0, three0, one1, three1 = attend(
        after(info, two0), (0, 1), (1, 3), [after0, before0, after1, before1], keys, values
    )
    scan_inputs = (
        mine, conv_state_x, conv_state_bc, conv_weight_x, conv_bias_x, conv_weight_bc, conv_bias_bc,
        dt_bias, a_log, skip_d, ssm_state,
    )
    scanned = state_space(position, *after(scan_inputs, one0))
    back = lax.all_to_all(scanned, "ctx", 0, 0, tiled=True)
    two0, two1 = moves[1](two0, 2), moves[0](two1, 2)
    side0 = [moves[1](one0, 1), moves[1](three0, -1)]
    one1, three1 = after((one1, three1), (two0, two1))
    side1 = [moves[0](one1, 1), moves[0](three1, -1)]
    blocks0 = merge([after(own0, scanned), *side0, two0])
    home0 = [blocks0[0], *sent_home(*blocks0[1:], "x")]
    blocks1 = merge([after(own1, blocks0[0]), *side1, two1])
    blocks1 = after(blocks1, back)
    home1 = [blocks1[0], *sent_home(*blocks1[1:], "y")]
    return finish(home0, home1), unpacked(back)


def solution(mesh):
    token = P("dp", "ctx", "head")
    placed = (
        token, token, token, token, token, P("dp"), token, P("dp", "ctx", None), token,
        P("dp", None, "head"), P("dp", None, None), P(None, "head"), P("head"), P(), P(),
        P("head"), P("head"), P("head"), P("dp", "head", None, None),
    )
    return jax.shard_map(
        per_device, mesh=mesh, in_specs=placed, out_specs=(token, token), check_vma=False
    )
```

```python
import functools
import math

import jax
import jax.numpy as jnp
from jax import lax
from jax.experimental import pallas as pl
from jax.experimental.pallas import tpu as pltpu
from jax.sharding import PartitionSpec as P

HD = 224
PAD = 256
L_LANE = 224
M_LANE = 226
NEG_FILL = -1e30
EMPTY_TOP = -8192.0
HIGHEST = lax.Precision.HIGHEST
BF = jnp.bfloat16
F32 = jnp.float32
SIDE = 4
MIB = 1024 * 1024


def params(mib=16):
    return pltpu.CompilerParams(vmem_limit_bytes=mib * MIB)


def shifted(value, dy, dx):
    pairs = [
        (y * SIDE + x, ((y + dy) % SIDE) * SIDE + (x + dx) % SIDE)
        for y in range(SIDE)
        for x in range(SIDE)
    ]
    return lax.ppermute(value, "ctx", pairs)


def along(axis):
    if axis == "x":
        return lambda value, step: shifted(value, 0, step)
    return lambda value, step: shifted(value, step, 0)


def widened(block, extra):
    return jnp.concatenate([block, extra], axis=1)


def pad_cache(info, request, k_ref, gk_ref, v_ref, gv_ref, ko_ref, vo_ref):
    rows = k_ref.shape[1]
    group_rows = gk_ref.shape[1]
    first = lax.axis_index("ctx") * rows
    length = info[request]
    lane = lax.broadcasted_iota(jnp.int32, (rows, PAD - HD), 1)
    row = lax.broadcasted_iota(jnp.int32, (rows, PAD - HD), 0)
    cache_bias = jnp.where((lane == 0) & (first + row >= length), NEG_FILL, 0.0).astype(BF)
    group_bias = jnp.zeros((group_rows, PAD - HD), BF)
    ones = jnp.where(lane == 0, 1.0, 0.0).astype(BF)
    for h in range(ko_ref.shape[1]):
        window = slice(h * HD, (h + 1) * HD)
        ko_ref[0, h, :rows, :] = widened(k_ref[0, :, window], cache_bias)
        ko_ref[0, h, rows:, :] = widened(gk_ref[0, :, window], group_bias)
        vo_ref[0, h, :rows, :] = widened(v_ref[0, :, window], ones)
        vo_ref[0, h, rows:, :] = widened(gv_ref[0, :, window], ones[:group_rows])


def attend_kernel(requests, groups, pads, info, *refs):
    sets = len(groups)
    count = len(requests) * sets
    q_refs, refs = refs[:count], refs[count:]
    if pads:
        raw, refs = refs[:4], refs[4:]
        outs, (k_ref, v_ref) = refs[:count], refs[count:]
    else:
        (k_ref, v_ref), outs = refs[:2], refs[2:]
    turn = pl.program_id(0)
    here = k_ref.shape[1]
    span = q_refs[0].shape[0]
    rows = sets * span
    block = 64
    cached = k_ref.shape[2] - block
    scale = math.log2(math.e) / math.sqrt(HD)
    if pads:
        pad_cache(info, turn, *raw, k_ref, v_ref)
    position = lax.axis_index("ctx")

    def body(n):
        row = lax.broadcasted_iota(jnp.int32, (block, block), 0)
        col = lax.broadcasted_iota(jnp.int32, (block, block), 1) + position * block
        masks = []
        for group in groups:
            for lap in range(SIDE):
                along_y, along_x = (group, lap) if requests[n] == 0 else (lap, group)
                source = ((position // SIDE + along_y) % SIDE) * SIDE + (position % SIDE + along_x) % SIDE
                masks.append(col <= row + source * block)
        allowed = jnp.concatenate(masks, axis=0)
        lane = lax.broadcasted_iota(jnp.int32, (rows, PAD), 1)
        mine = q_refs[n * sets : (n + 1) * sets]

        def scored(i):
            queries = [ref[:, i * PAD : (i + 1) * PAD] for ref in mine]
            return lax.dot_general(
                jnp.concatenate(queries, axis=0) if sets > 1 else queries[0],
                k_ref[0, i],
                (((1,), (1,)), ((), ())),
                preferred_element_type=F32,
            )

        def store(i, scores):
            tail = jnp.where(allowed, scores[:, cached:], NEG_FILL)
            scores = jnp.concatenate([scores[:, :cached], tail], axis=1)
            top = jnp.maximum(jnp.max(scores, axis=1, keepdims=True) * scale, EMPTY_TOP)
            top = jnp.round(top).astype(BF).astype(F32)
            weights = jnp.exp2(scores * scale - top).astype(BF)
            out = jnp.dot(weights, v_ref[0, i], preferred_element_type=F32)
            out = jnp.where(lane == M_LANE, top, out).astype(BF)
            for at in range(sets):
                outs[n * sets + at][:, i * PAD : (i + 1) * PAD] = out[at * span : (at + 1) * span]

        scores = scored(0)
        for i in range(here):
            following = scored(i + 1) if i + 1 < here else None
            store(i, scores)
            scores = following

    for n in range(len(requests)):
        if len(requests) == 1:
            body(n)
        else:
            pl.when(turn == n)(functools.partial(body, n))


def attend(info, requests, groups, queries, keys, values, raw=None):
    sets = len(groups)
    span, width = queries[0].shape
    rows = sets * span
    heads = width // PAD
    steps = 2
    here = heads // steps
    if raw is None:
        _, _, total, _ = keys.shape
    else:
        _, cached, _ = raw[0].shape
        group_rows = raw[1].shape[1]
        total = cached + group_rows
    base = requests[0]

    def column(n):
        def at(r, g, s):
            return 0, jnp.where(r == n, g, jnp.where(r < n, 0, steps - 1))

        return at

    kv = pl.BlockSpec((1, here, total, PAD), lambda r, g, s: (base + r, g, 0, 0))
    order = [n for n in range(len(requests)) for _ in range(sets)]
    ins = [pl.BlockSpec((span, here * PAD), column(n)) for n in order]
    outs = [pl.BlockSpec((span, here * PAD), column(n)) for n in order]
    shapes = [jax.ShapeDtypeStruct((span, heads * PAD), BF)] * len(order)
    moved = 9_000_000 * len(requests) + 6 * len(requests) * rows * width
    if raw is None:
        operands, specs = [keys, values], [kv, kv]
    else:
        operands = list(raw)
        wide = pl.BlockSpec((1, cached, here * HD), lambda r, g, s: (r, 0, g))
        small = pl.BlockSpec((1, group_rows, here * HD), lambda r, g, s: (r, 0, g))
        specs = [wide, small, wide, small]
        outs += [kv, kv]
        shapes += [jax.ShapeDtypeStruct((len(requests), heads, total, PAD), BF)] * 2
        moved += 16_000_000
    work = len(requests) * heads * rows * total
    return pl.pallas_call(
        functools.partial(attend_kernel, requests, groups, raw is not None),
        grid_spec=pltpu.PrefetchScalarGridSpec(
            num_scalar_prefetch=1,
            grid=(len(requests), steps),
            in_specs=[*ins, *specs],
            out_specs=outs,
        ),
        out_shape=shapes,
        compiler_params=params(44 if raw is None and sets == 1 else 56),
        cost_estimate=pl.CostEstimate(flops=6 * work * PAD, bytes_accessed=moved, transcendentals=work),
        name="attend",
    )(info, *queries, *operands)


def join_kernel(own_ref, *refs):
    outs = refs[6:]
    rows = own_ref.shape[1]
    lane = lax.broadcasted_iota(jnp.int32, (rows, PAD - HD), 1)
    ones = jnp.where(lane == 0, 1.0, 0.0).astype(BF)
    for r, out in enumerate(outs):
        blocks = [own_ref.at[r], *refs[3 * r : 3 * r + 3]]
        for n, ref in enumerate(blocks):
            for h in range(own_ref.shape[2] // HD):
                out[n * rows : (n + 1) * rows, h * PAD : (h + 1) * PAD] = widened(
                    ref[:, h * HD : (h + 1) * HD], ones
                )


def joined_rows(own, others0, others1):
    _, rows, width = own.shape
    padded = width // HD * PAD
    return pl.pallas_call(
        join_kernel,
        out_shape=[jax.ShapeDtypeStruct((SIDE * rows, padded), BF)] * 2,
        compiler_params=params(),
        cost_estimate=pl.CostEstimate(flops=0, bytes_accessed=16 * rows * width * 2, transcendentals=0),
        name="join",
    )(own, *others0, *others1)


def merged(parts):
    tops = [part[:, M_LANE : M_LANE + 1] for part in parts]
    top = functools.reduce(jnp.maximum, tops)
    return sum(part * jnp.exp2(own - top) for part, own in zip(parts, tops)), top


def merge_kernel(*refs):
    parts, outs = refs[:4], refs[4:]
    rows = outs[0].shape[0]
    lane = lax.broadcasted_iota(jnp.int32, (rows, PAD), 1)
    for h in range(outs[0].shape[1] // PAD):
        window = slice(h * PAD, (h + 1) * PAD)
        for b in range(SIDE):
            at = slice(b * rows, (b + 1) * rows)
            total, top = merged([ref[at, window].astype(F32) for ref in parts])
            outs[b][:, window] = jnp.where(lane == M_LANE, top, total).astype(BF)


def merge(parts):
    rows, width = parts[0].shape
    steps = 2
    spec = pl.BlockSpec((rows, width // steps), lambda i: (0, i))
    out = pl.BlockSpec((rows // SIDE, width // steps), lambda i: (0, i))
    return pl.pallas_call(
        merge_kernel,
        grid=(steps,),
        in_specs=[spec] * 4,
        out_specs=[out] * 4,
        out_shape=[jax.ShapeDtypeStruct((rows // SIDE, width), BF)] * 4,
        compiler_params=params(56),
        cost_estimate=pl.CostEstimate(
            flops=rows * width * 8, bytes_accessed=rows * width * 10, transcendentals=0
        ),
        name="merge",
    )(*parts)


def finish_kernel(count, *refs):
    out_ref = refs[2 * count]
    heads = out_ref.shape[2] // HD
    for r in range(2):
        done = []
        for h in range(heads):
            window = slice(h * PAD, (h + 1) * PAD)
            total, _ = merged([ref[:, window].astype(F32) for ref in refs[r * count : (r + 1) * count]])
            done.append((total / total[:, L_LANE : L_LANE + 1])[:, :HD])
        out_ref[r] = jnp.concatenate(done, axis=1).astype(BF)


def finish(parts0, parts1):
    rows, width = parts0[0].shape
    heads = width // PAD
    return pl.pallas_call(
        functools.partial(finish_kernel, len(parts0)),
        out_shape=jax.ShapeDtypeStruct((2, rows, heads * HD), BF),
        compiler_params=params(),
        cost_estimate=pl.CostEstimate(
            flops=rows * width * 16, bytes_accessed=rows * width * 20, transcendentals=0
        ),
        name="finish",
    )(*parts0, *parts1)


def pack_kernel(x_ref, dt_ref, bc_ref, out_ref):
    rows = x_ref.shape[1]
    heads = dt_ref.shape[2]
    for r in range(2):
        extra = jnp.concatenate([dt_ref[r], jnp.zeros((rows, PAD - HD - heads), BF)], axis=1)
        for c in range(8):
            out_ref[r * 8 + c, :, :PAD] = jnp.concatenate(
                [x_ref[r, :, c * HD : (c + 1) * HD], extra], axis=1
            )
            out_ref[r * 8 + c, :, PAD:] = bc_ref[r]


def unpack_kernel(in_ref, out_ref):
    for r in range(2):
        out_ref[r] = jnp.concatenate(
            [in_ref[r * 8 + c].astype(F32)[:, :HD] for c in range(8)], axis=1
        ).astype(BF)


def split(value):
    high = value.astype(BF)
    return high, (value - high.astype(F32)).astype(BF)


def split_three(value):
    high = value.astype(BF)
    rest = value - high.astype(F32)
    middle, low = split(rest)
    return high, middle, low


def scan_kernel(
    info, data_ref, cx_ref, wx_ref, bx_ref, cb_ref, wb_ref, bb_ref, head_ref, state_ref, out_ref,
    xs_ref, bcs_ref, par_ref,
):
    tokens = data_ref.shape[0]
    chunk = 128
    request, start = info[0], info[1]
    first_head = (7 * start) // 2
    taps = wx_ref.shape[0]
    rim = taps - 1
    before = 8 - rim
    for c in range(8):

        @pl.when(start == c)
        def _():
            window = slice(c * HD, (c + 1) * HD)
            par_ref[0:taps, :HD] = wx_ref[:, window]
            par_ref[taps : taps + 1, :HD] = bx_ref[:, window]
            xs_ref[before:8, :HD] = cx_ref[request].astype(F32)[:, window]

    par_ref[:, HD:] = jnp.zeros((8, PAD - HD), F32)
    xs_ref[0:8, HD:] = jnp.zeros((8, PAD - HD), F32)
    bcs_ref[before:8, :] = cb_ref[request].astype(F32)
    xs_ref[8:, :] = data_ref[:, :PAD].astype(F32)
    bcs_ref[8:, :] = data_ref[:, PAD:].astype(F32)

    lane = lax.broadcasted_iota(jnp.int32, (8, PAD), 1) + start * HD
    head = lax.broadcasted_iota(jnp.int32, (8, PAD), 0) + first_head
    spread = (lane // 64 == head).astype(F32)
    spread3 = jnp.concatenate([spread] * 3, axis=0).astype(BF)
    pick = (
        lax.broadcasted_iota(jnp.int32, (128, 8), 0)
        == lax.broadcasted_iota(jnp.int32, (128, 8), 1) + (HD - 128) + first_head
    ).astype(F32)
    headpar = jnp.dot(head_ref[...], pick, precision=HIGHEST, preferred_element_type=F32)
    dt_bias, rate, skip = headpar[0:1], jnp.exp(headpar[1:2]), headpar[2:3]
    skip_wide = jnp.dot(skip, spread, precision=HIGHEST, preferred_element_type=F32)
    row = lax.broadcasted_iota(jnp.int32, (chunk, chunk), 0)
    col = lax.broadcasted_iota(jnp.int32, (chunk, chunk), 1)
    lower = row >= col
    lower_b = lower.astype(F32).astype(BF)
    pick_b = pick.astype(BF)
    masks = [spread[h : h + 1] for h in range(4)]
    state = jnp.concatenate(
        [state_ref[0, pl.ds(pl.multiple_of(start * HD, 32), HD), :], jnp.zeros((PAD - HD, 64), F32)], axis=0
    ).T
    for c in range(tokens // chunk):
        at = c * chunk
        x = jnp.zeros((chunk, PAD), F32) + par_ref[taps : taps + 1, :]
        bc = jnp.zeros((chunk, 128), F32) + bb_ref[...]
        for i in range(taps):
            x = x + par_ref[i : i + 1, :] * xs_ref[at + before + i : at + before + i + chunk, :]
            bc = bc + wb_ref[i : i + 1, :] * bcs_ref[at + before + i : at + before + i + chunk, :]
        x = x * jax.nn.sigmoid(x)
        bc = bc * jax.nn.sigmoid(bc)
        b, o = bc[:, :64], bc[:, 64:]
        raw = data_ref[at : at + chunk, 128:PAD]
        size = jnp.dot(raw, pick_b, preferred_element_type=F32) + dt_bias
        size = jnp.maximum(size, 0.0) + jnp.log1p(jnp.exp(-jnp.abs(size)))
        run = jnp.dot(
            lower_b, jnp.concatenate(split_three(-rate * size), axis=1), preferred_element_type=F32
        )
        run = run[:, :8] + run[:, 8:16] + run[:, 16:24]
        run_t = run.T
        wide = jnp.dot(
            jnp.concatenate(split_three(jnp.concatenate([size, run], axis=0)), axis=1),
            spread3,
            preferred_element_type=F32,
        )
        size_wide, run_wide = wide[:chunk], wide[chunk:]
        xdt = x * size_wide
        o_high, o_low = split(o)
        b_high, b_low = split(b)
        o_three = jnp.concatenate([o_high, o_high, o_low], axis=1)
        cross = lax.dot_general(
            o_three,
            jnp.concatenate([b_high, b_low, b_high], axis=1),
            (((1,), (1,)), ((), ())),
            preferred_element_type=F32,
        )
        pieces, mixes = [], []
        for h in range(4):
            gap = run[:, h : h + 1] - run_t[h : h + 1, :]
            mixes.append((jnp.exp(jnp.where(lower, gap, NEG_FILL)) * cross).astype(BF))
            pieces.append((xdt * masks[h]).astype(BF))
        y = jnp.dot(
            jnp.concatenate(mixes, axis=1), jnp.concatenate(pieces, axis=0), preferred_element_type=F32
        )
        s_high, s_low = split(state)
        y = y + jnp.exp(run_wide) * jnp.dot(
            o_three, jnp.concatenate([s_high, s_low, s_high], axis=0), preferred_element_type=F32
        )
        last = run_wide[chunk - 1 : chunk]
        w_high, w_low = split(xdt * jnp.exp(last - run_wide))
        state = state * jnp.exp(last) + lax.dot_general(
            jnp.concatenate([b_high, b_high, b_low], axis=0),
            jnp.concatenate([w_high, w_low, w_high], axis=0),
            (((0,), (0,)), ((), ())),
            preferred_element_type=F32,
        )
        out_ref[at : at + chunk, :] = (y + skip_wide * x).astype(BF)


def channels_in(mamba_x, mamba_bc, mamba_dt):
    rows = mamba_x.shape[1]
    packed = pl.pallas_call(
        pack_kernel,
        out_shape=jax.ShapeDtypeStruct((16, rows, PAD + 128), BF),
        compiler_params=params(),
        name="pack",
    )(mamba_x, mamba_dt, mamba_bc)
    return packed, lax.all_to_all(packed, "ctx", 0, 0, tiled=True).reshape(16 * rows, PAD + 128)


def state_space(
    position, mine, conv_state_x, conv_state_bc, conv_weight_x, conv_bias_x, conv_weight_bc,
    conv_bias_bc, dt_bias, a_log, skip_d, ssm_state,
):
    rows = mine.shape[0] // 16
    heads = dt_bias.shape[0]
    headpar = jnp.pad(jnp.stack([dt_bias, a_log, skip_d]), ((0, 5), (HD - 128, 128 - (HD - 128) - heads)))
    state = ssm_state.reshape(2, -1, 64)
    tokens = 16 * rows

    def whole(value):
        return pl.BlockSpec(value.shape, lambda i, s: (0,) * value.ndim)

    operands = (
        mine, conv_state_x, conv_weight_x, conv_bias_x[None], conv_state_bc, conv_weight_bc,
        conv_bias_bc[None], headpar,
    )
    out = pl.pallas_call(
        scan_kernel,
        grid_spec=pltpu.PrefetchScalarGridSpec(
            num_scalar_prefetch=1,
            grid=(1,),
            in_specs=[*map(whole, operands), pl.BlockSpec((1, *state.shape[1:]), lambda i, s: (s[0], 0, 0))],
            out_specs=pl.BlockSpec((tokens, PAD), lambda i, s: (0, 0)),
            scratch_shapes=[
                pltpu.VMEM((tokens + 8, PAD), F32),
                pltpu.VMEM((tokens + 8, 128), F32),
                pltpu.VMEM((8, PAD), F32),
            ],
        ),
        out_shape=jax.ShapeDtypeStruct((tokens, PAD), BF),
        compiler_params=params(28),
        cost_estimate=pl.CostEstimate(
            flops=8_000_000_000, bytes_accessed=2_500_000, transcendentals=2_000_000
        ),
        name="scan",
    )(jnp.stack([position // 8, position % 8]).astype(jnp.int32), *operands, state)
    return out.reshape(16, rows, PAD)


def unpacked(back):
    return pl.pallas_call(
        unpack_kernel,
        out_shape=jax.ShapeDtypeStruct((2, back.shape[1], 8 * HD), BF),
        compiler_params=params(),
        name="unpack",
    )(back)


def after(values, done):
    return lax.optimization_barrier((values, done))[0]


def sent_home(one, two, three, axis):
    move = along(axis)
    return [move(one, 1), move(three, -1), move(two, 2)]


def per_device(
    group_queries, group_keys, group_values, cache_keys, cache_values, cache_lengths, mamba_x, mamba_bc,
    mamba_dt, conv_state_x, conv_state_bc, conv_weight_x, conv_bias_x, conv_weight_bc, conv_bias_bc,
    dt_bias, a_log, skip_d, ssm_state,
):
    position = lax.axis_index("ctx")
    info = cache_lengths
    queries = [group_queries[0], group_queries[1]]
    moves = [along("x"), along("y")]
    others = [[move(q, -1), move(q, 2), move(q, 1)] for q, move in zip(queries, moves)]
    packed, mine = channels_in(after(mamba_x, others[0][0]), mamba_bc, mamba_dt)
    first0, first1 = joined_rows(after(group_queries, packed), *others)
    far0, far1 = moves[1](first0, 2), moves[0](first1, 2)
    own0, own1, keys, values = attend(
        info, (0, 1), (0,), [first0, first1], None, None,
        (cache_keys, group_keys, cache_values, group_values),
    )
    first0, first1 = after((first0, first1), (far0, far1, own0))
    after0, before0 = moves[1](first0, -1), moves[1](first0, 1)
    after1, before1 = moves[0](first1, -1), moves[0](first1, 1)
    two0, two1 = attend(after(info, (own0, mine)), (0, 1), (2,), [far0, far1], keys, values)
    two0, two1 = after((two0, two1), (after0, before0, after1, before1))
    one0, three0, one1, three1 = attend(
        after(info, two0), (0, 1), (1, 3), [after0, before0, after1, before1], keys, values
    )
    scan_inputs = (
        mine, conv_state_x, conv_state_bc, conv_weight_x, conv_bias_x, conv_weight_bc, conv_bias_bc,
        dt_bias, a_log, skip_d, ssm_state,
    )
    scanned = state_space(position, *after(scan_inputs, one0))
    back = lax.all_to_all(scanned, "ctx", 0, 0, tiled=True)
    two0, two1 = moves[1](two0, 2), moves[0](two1, 2)
    side0 = [moves[1](one0, 1), moves[1](three0, -1)]
    three1 = after(three1, (two0, two1))
    side1 = [moves[0](one1, 1), moves[0](three1, -1)]
    blocks0 = merge([after(own0, scanned), *side0, two0])
    home0 = [blocks0[0], *sent_home(*blocks0[1:], "x")]
    blocks1 = merge([after(own1, blocks0[0]), *side1, two1])
    blocks1 = after(blocks1, back)
    home1 = [blocks1[0], *sent_home(*blocks1[1:], "y")]
    return finish(home0, home1), unpacked(back)


def solution(mesh):
    token = P("dp", "ctx", "head")
    placed = (
        token, token, token, token, token, P("dp"), token, P("dp", "ctx", None), token,
        P("dp", None, "head"), P("dp", None, None), P(None, "head"), P("head"), P(), P(),
        P("head"), P("head"), P("head"), P("dp", "head", None, None),
    )
    return jax.shard_map(
        per_device, mesh=mesh, in_specs=placed, out_specs=(token, token), check_vma=False
    )
```

```python
import functools
import math

import jax
import jax.numpy as jnp
from jax import lax
from jax.experimental import pallas as pl
from jax.experimental.pallas import tpu as pltpu
from jax.sharding import PartitionSpec as P

HD = 224
PAD = 256
L_LANE = 224
M_LANE = 226
NEG_FILL = -1e30
EMPTY_TOP = -8192.0
HIGHEST = lax.Precision.HIGHEST
BF = jnp.bfloat16
F32 = jnp.float32
SIDE = 4
MIB = 1024 * 1024


def params(mib=16):
    return pltpu.CompilerParams(vmem_limit_bytes=mib * MIB)


def shifted(value, dy, dx):
    pairs = [
        (y * SIDE + x, ((y + dy) % SIDE) * SIDE + (x + dx) % SIDE)
        for y in range(SIDE)
        for x in range(SIDE)
    ]
    return lax.ppermute(value, "ctx", pairs)


def along(axis):
    if axis == "x":
        return lambda value, step: shifted(value, 0, step)
    return lambda value, step: shifted(value, step, 0)


def widened(block, extra):
    return jnp.concatenate([block, extra], axis=1)


def pad_cache(info, request, k_ref, gk_ref, v_ref, gv_ref, ko_ref, vo_ref):
    rows = k_ref.shape[1]
    group_rows = gk_ref.shape[1]
    first = lax.axis_index("ctx") * rows
    length = info[request]
    lane = lax.broadcasted_iota(jnp.int32, (rows, PAD - HD), 1)
    row = lax.broadcasted_iota(jnp.int32, (rows, PAD - HD), 0)
    cache_bias = jnp.where((lane == 0) & (first + row >= length), NEG_FILL, 0.0).astype(BF)
    group_bias = jnp.zeros((group_rows, PAD - HD), BF)
    ones = jnp.where(lane == 0, 1.0, 0.0).astype(BF)
    for h in range(ko_ref.shape[1]):
        window = slice(h * HD, (h + 1) * HD)
        ko_ref[0, h, :rows, :] = widened(k_ref[0, :, window], cache_bias)
        ko_ref[0, h, rows:, :] = widened(gk_ref[0, :, window], group_bias)
        vo_ref[0, h, :rows, :] = widened(v_ref[0, :, window], ones)
        vo_ref[0, h, rows:, :] = widened(gv_ref[0, :, window], ones[:group_rows])


def attend_kernel(requests, groups, pads, info, *refs):
    sets = len(groups)
    count = len(requests) * sets
    q_refs, refs = refs[:count], refs[count:]
    if pads:
        raw, refs = refs[:4], refs[4:]
        outs, (k_ref, v_ref) = refs[:count], refs[count:]
    else:
        (k_ref, v_ref), outs = refs[:2], refs[2:]
    turn = pl.program_id(0)
    here = k_ref.shape[1]
    span = q_refs[0].shape[0]
    rows = sets * span
    block = 64
    cached = k_ref.shape[2] - block
    scale = math.log2(math.e) / math.sqrt(HD)
    if pads:
        pad_cache(info, turn, *raw, k_ref, v_ref)
    position = lax.axis_index("ctx")

    def body(n):
        row = lax.broadcasted_iota(jnp.int32, (block, block), 0)
        col = lax.broadcasted_iota(jnp.int32, (block, block), 1) + position * block
        masks = []
        for group in groups:
            for lap in range(SIDE):
                along_y, along_x = (group, lap) if requests[n] == 0 else (lap, group)
                source = ((position // SIDE + along_y) % SIDE) * SIDE + (position % SIDE + along_x) % SIDE
                masks.append(col <= row + source * block)
        allowed = jnp.concatenate(masks, axis=0)
        lane = lax.broadcasted_iota(jnp.int32, (rows, PAD), 1)
        mine = q_refs[n * sets : (n + 1) * sets]

        def scored(i):
            queries = [ref[:, i * PAD : (i + 1) * PAD] for ref in mine]
            return lax.dot_general(
                jnp.concatenate(queries, axis=0) if sets > 1 else queries[0],
                k_ref[0, i],
                (((1,), (1,)), ((), ())),
                preferred_element_type=F32,
            )

        def store(i, scores):
            tail = jnp.where(allowed, scores[:, cached:], NEG_FILL)
            scores = jnp.concatenate([scores[:, :cached], tail], axis=1)
            top = jnp.maximum(jnp.max(scores, axis=1, keepdims=True) * scale, EMPTY_TOP)
            top = jnp.round(top).astype(BF).astype(F32)
            weights = jnp.exp2(scores * scale - top).astype(BF)
            out = jnp.dot(weights, v_ref[0, i], preferred_element_type=F32)
            out = jnp.where(lane == M_LANE, top, out).astype(BF)
            for at in range(sets):
                outs[n * sets + at][:, i * PAD : (i + 1) * PAD] = out[at * span : (at + 1) * span]

        scores = scored(0)
        for i in range(here):
            following = scored(i + 1) if i + 1 < here else None
            store(i, scores)
            scores = following

    for n in range(len(requests)):
        if len(requests) == 1:
            body(n)
        else:
            pl.when(turn == n)(functools.partial(body, n))


def attend(info, requests, groups, queries, keys, values, raw=None):
    sets = len(groups)
    span, width = queries[0].shape
    rows = sets * span
    heads = width // PAD
    steps = 2
    here = heads // steps
    if raw is None:
        _, _, total, _ = keys.shape
    else:
        _, cached, _ = raw[0].shape
        group_rows = raw[1].shape[1]
        total = cached + group_rows
    base = requests[0]

    def column(n):
        def at(r, g, s):
            return 0, jnp.where(r == n, g, jnp.where(r < n, 0, steps - 1))

        return at

    kv = pl.BlockSpec((1, here, total, PAD), lambda r, g, s: (base + r, g, 0, 0))
    order = [n for n in range(len(requests)) for _ in range(sets)]
    ins = [pl.BlockSpec((span, here * PAD), column(n)) for n in order]
    outs = [pl.BlockSpec((span, here * PAD), column(n)) for n in order]
    shapes = [jax.ShapeDtypeStruct((span, heads * PAD), BF)] * len(order)
    moved = 9_000_000 * len(requests) + 6 * len(requests) * rows * width
    if raw is None:
        operands, specs = [keys, values], [kv, kv]
    else:
        operands = list(raw)
        wide = pl.BlockSpec((1, cached, here * HD), lambda r, g, s: (r, 0, g))
        small = pl.BlockSpec((1, group_rows, here * HD), lambda r, g, s: (r, 0, g))
        specs = [wide, small, wide, small]
        outs += [kv, kv]
        shapes += [jax.ShapeDtypeStruct((len(requests), heads, total, PAD), BF)] * 2
        moved += 16_000_000
    work = len(requests) * heads * rows * total
    return pl.pallas_call(
        functools.partial(attend_kernel, requests, groups, raw is not None),
        grid_spec=pltpu.PrefetchScalarGridSpec(
            num_scalar_prefetch=1,
            grid=(len(requests), steps),
            in_specs=[*ins, *specs],
            out_specs=outs,
        ),
        out_shape=shapes,
        compiler_params=params(44 if raw is None and sets == 1 else 56),
        cost_estimate=pl.CostEstimate(flops=6 * work * PAD, bytes_accessed=moved, transcendentals=work),
        name="attend",
    )(info, *queries, *operands)


def join_kernel(own_ref, *refs):
    outs = refs[6:]
    rows = own_ref.shape[1]
    lane = lax.broadcasted_iota(jnp.int32, (rows, PAD - HD), 1)
    ones = jnp.where(lane == 0, 1.0, 0.0).astype(BF)
    for r, out in enumerate(outs):
        blocks = [own_ref.at[r], *refs[3 * r : 3 * r + 3]]
        for n, ref in enumerate(blocks):
            for h in range(own_ref.shape[2] // HD):
                out[n * rows : (n + 1) * rows, h * PAD : (h + 1) * PAD] = widened(
                    ref[:, h * HD : (h + 1) * HD], ones
                )


def joined_rows(own, others0, others1):
    _, rows, width = own.shape
    padded = width // HD * PAD
    return pl.pallas_call(
        join_kernel,
        out_shape=[jax.ShapeDtypeStruct((SIDE * rows, padded), BF)] * 2,
        compiler_params=params(),
        cost_estimate=pl.CostEstimate(flops=0, bytes_accessed=16 * rows * width * 2, transcendentals=0),
        name="join",
    )(own, *others0, *others1)


def merged(parts):
    tops = [part[:, M_LANE : M_LANE + 1] for part in parts]
    top = functools.reduce(jnp.maximum, tops)
    return sum(part * jnp.exp2(own - top) for part, own in zip(parts, tops)), top


def merge_kernel(*refs):
    parts, outs = refs[:4], refs[4:]
    rows = outs[0].shape[0]
    lane = lax.broadcasted_iota(jnp.int32, (rows, PAD), 1)
    for h in range(outs[0].shape[1] // PAD):
        window = slice(h * PAD, (h + 1) * PAD)
        for b in range(SIDE):
            at = slice(b * rows, (b + 1) * rows)
            total, top = merged([ref[at, window].astype(F32) for ref in parts])
            outs[b][:, window] = jnp.where(lane == M_LANE, top, total).astype(BF)


def merge(parts):
    rows, width = parts[0].shape
    steps = 2
    spec = pl.BlockSpec((rows, width // steps), lambda i: (0, i))
    out = pl.BlockSpec((rows // SIDE, width // steps), lambda i: (0, i))
    return pl.pallas_call(
        merge_kernel,
        grid=(steps,),
        in_specs=[spec] * 4,
        out_specs=[out] * 4,
        out_shape=[jax.ShapeDtypeStruct((rows // SIDE, width), BF)] * 4,
        compiler_params=params(56),
        cost_estimate=pl.CostEstimate(
            flops=rows * width * 8, bytes_accessed=rows * width * 10, transcendentals=0
        ),
        name="merge",
    )(*parts)


def finish_kernel(count, *refs):
    out_ref = refs[2 * count]
    heads = out_ref.shape[2] // HD
    for r in range(2):
        done = []
        for h in range(heads):
            window = slice(h * PAD, (h + 1) * PAD)
            total, _ = merged([ref[:, window].astype(F32) for ref in refs[r * count : (r + 1) * count]])
            done.append((total / total[:, L_LANE : L_LANE + 1])[:, :HD])
        out_ref[r] = jnp.concatenate(done, axis=1).astype(BF)


def finish(parts0, parts1):
    rows, width = parts0[0].shape
    heads = width // PAD
    return pl.pallas_call(
        functools.partial(finish_kernel, len(parts0)),
        out_shape=jax.ShapeDtypeStruct((2, rows, heads * HD), BF),
        compiler_params=params(),
        cost_estimate=pl.CostEstimate(
            flops=rows * width * 16, bytes_accessed=rows * width * 20, transcendentals=0
        ),
        name="finish",
    )(*parts0, *parts1)


def pack_kernel(x_ref, dt_ref, bc_ref, out_ref):
    rows = x_ref.shape[1]
    heads = dt_ref.shape[2]
    for r in range(2):
        extra = jnp.concatenate([dt_ref[r], jnp.zeros((rows, PAD - HD - heads), BF)], axis=1)
        for c in range(8):
            out_ref[r * 8 + c, :, :PAD] = jnp.concatenate(
                [x_ref[r, :, c * HD : (c + 1) * HD], extra], axis=1
            )
            out_ref[r * 8 + c, :, PAD:] = bc_ref[r]


def unpack_kernel(in_ref, out_ref):
    for r in range(2):
        out_ref[r] = jnp.concatenate(
            [in_ref[r * 8 + c].astype(F32)[:, :HD] for c in range(8)], axis=1
        ).astype(BF)


def split(value):
    high = value.astype(BF)
    return high, (value - high.astype(F32)).astype(BF)


def split_three(value):
    high = value.astype(BF)
    rest = value - high.astype(F32)
    middle, low = split(rest)
    return high, middle, low


def scan_kernel(
    info, data_ref, cx_ref, wx_ref, bx_ref, cb_ref, wb_ref, bb_ref, head_ref, state_ref, out_ref,
    xs_ref, bcs_ref, par_ref,
):
    tokens = data_ref.shape[0]
    chunk = 128
    request, start = info[0], info[1]
    first_head = (7 * start) // 2
    taps = wx_ref.shape[0]
    rim = taps - 1
    before = 8 - rim
    for c in range(8):

        @pl.when(start == c)
        def _():
            window = slice(c * HD, (c + 1) * HD)
            par_ref[0:taps, :HD] = wx_ref[:, window]
            par_ref[taps : taps + 1, :HD] = bx_ref[:, window]
            xs_ref[before:8, :HD] = cx_ref[request].astype(F32)[:, window]

    par_ref[:, HD:] = jnp.zeros((8, PAD - HD), F32)
    xs_ref[0:8, HD:] = jnp.zeros((8, PAD - HD), F32)
    bcs_ref[before:8, :] = cb_ref[request].astype(F32)
    xs_ref[8:, :] = data_ref[:, :PAD].astype(F32)
    bcs_ref[8:, :] = data_ref[:, PAD:].astype(F32)

    lane = lax.broadcasted_iota(jnp.int32, (8, PAD), 1) + start * HD
    head = lax.broadcasted_iota(jnp.int32, (8, PAD), 0) + first_head
    spread = (lane // 64 == head).astype(F32)
    spread3 = jnp.concatenate([spread] * 3, axis=0).astype(BF)
    pick = (
        lax.broadcasted_iota(jnp.int32, (128, 8), 0)
        == lax.broadcasted_iota(jnp.int32, (128, 8), 1) + (HD - 128) + first_head
    ).astype(F32)
    headpar = jnp.dot(head_ref[...], pick, precision=HIGHEST, preferred_element_type=F32)
    dt_bias, rate, skip = headpar[0:1], jnp.exp(headpar[1:2]), headpar[2:3]
    skip_wide = jnp.dot(skip, spread, precision=HIGHEST, preferred_element_type=F32)
    row = lax.broadcasted_iota(jnp.int32, (chunk, chunk), 0)
    col = lax.broadcasted_iota(jnp.int32, (chunk, chunk), 1)
    lower = row >= col
    lower_b = lower.astype(F32).astype(BF)
    pick_b = pick.astype(BF)
    masks = [spread[h : h + 1] for h in range(4)]
    state = jnp.concatenate(
        [state_ref[0, pl.ds(pl.multiple_of(start * HD, 32), HD), :], jnp.zeros((PAD - HD, 64), F32)], axis=0
    ).T
    for c in range(tokens // chunk):
        at = c * chunk
        x = jnp.zeros((chunk, PAD), F32) + par_ref[taps : taps + 1, :]
        bc = jnp.zeros((chunk, 128), F32) + bb_ref[...]
        for i in range(taps):
            x = x + par_ref[i : i + 1, :] * xs_ref[at + before + i : at + before + i + chunk, :]
            bc = bc + wb_ref[i : i + 1, :] * bcs_ref[at + before + i : at + before + i + chunk, :]
        x = x * jax.nn.sigmoid(x)
        bc = bc * jax.nn.sigmoid(bc)
        b, o = bc[:, :64], bc[:, 64:]
        raw = data_ref[at : at + chunk, 128:PAD]
        size = jnp.dot(raw, pick_b, preferred_element_type=F32) + dt_bias
        size = jnp.maximum(size, 0.0) + jnp.log1p(jnp.exp(-jnp.abs(size)))
        run = jnp.dot(
            lower_b, jnp.concatenate(split_three(-rate * size), axis=1), preferred_element_type=F32
        )
        run = run[:, :8] + run[:, 8:16] + run[:, 16:24]
        run_t = run.T
        wide = jnp.dot(
            jnp.concatenate(split_three(jnp.concatenate([size, run], axis=0)), axis=1),
            spread3,
            preferred_element_type=F32,
        )
        size_wide, run_wide = wide[:chunk], wide[chunk:]
        xdt = x * size_wide
        o_high, o_low = split(o)
        b_high, b_low = split(b)
        o_three = jnp.concatenate([o_high, o_high, o_low], axis=1)
        cross = lax.dot_general(
            o_three,
            jnp.concatenate([b_high, b_low, b_high], axis=1),
            (((1,), (1,)), ((), ())),
            preferred_element_type=F32,
        )
        pieces, mixes = [], []
        for h in range(4):
            gap = run[:, h : h + 1] - run_t[h : h + 1, :]
            mixes.append((jnp.exp(jnp.where(lower, gap, NEG_FILL)) * cross).astype(BF))
            pieces.append((xdt * masks[h]).astype(BF))
        y = jnp.dot(
            jnp.concatenate(mixes, axis=1), jnp.concatenate(pieces, axis=0), preferred_element_type=F32
        )
        s_high, s_low = split(state)
        y = y + jnp.exp(run_wide) * jnp.dot(
            o_three, jnp.concatenate([s_high, s_low, s_high], axis=0), preferred_element_type=F32
        )
        last = run_wide[chunk - 1 : chunk]
        w_high, w_low = split(xdt * jnp.exp(last - run_wide))
        state = state * jnp.exp(last) + lax.dot_general(
            jnp.concatenate([b_high, b_high, b_low], axis=0),
            jnp.concatenate([w_high, w_low, w_high], axis=0),
            (((0,), (0,)), ((), ())),
            preferred_element_type=F32,
        )
        out_ref[at : at + chunk, :] = (y + skip_wide * x).astype(BF)


def channels_in(mamba_x, mamba_bc, mamba_dt):
    rows = mamba_x.shape[1]
    packed = pl.pallas_call(
        pack_kernel,
        out_shape=jax.ShapeDtypeStruct((16, rows, PAD + 128), BF),
        compiler_params=params(),
        name="pack",
    )(mamba_x, mamba_dt, mamba_bc)
    return packed, lax.all_to_all(packed, "ctx", 0, 0, tiled=True).reshape(16 * rows, PAD + 128)


def state_space(
    position, mine, conv_state_x, conv_state_bc, conv_weight_x, conv_bias_x, conv_weight_bc,
    conv_bias_bc, dt_bias, a_log, skip_d, ssm_state,
):
    rows = mine.shape[0] // 16
    heads = dt_bias.shape[0]
    headpar = jnp.pad(jnp.stack([dt_bias, a_log, skip_d]), ((0, 5), (HD - 128, 128 - (HD - 128) - heads)))
    state = ssm_state.reshape(2, -1, 64)
    tokens = 16 * rows

    def whole(value):
        return pl.BlockSpec(value.shape, lambda i, s: (0,) * value.ndim)

    operands = (
        mine, conv_state_x, conv_weight_x, conv_bias_x[None], conv_state_bc, conv_weight_bc,
        conv_bias_bc[None], headpar,
    )
    out = pl.pallas_call(
        scan_kernel,
        grid_spec=pltpu.PrefetchScalarGridSpec(
            num_scalar_prefetch=1,
            grid=(1,),
            in_specs=[*map(whole, operands), pl.BlockSpec((1, *state.shape[1:]), lambda i, s: (s[0], 0, 0))],
            out_specs=pl.BlockSpec((tokens, PAD), lambda i, s: (0, 0)),
            scratch_shapes=[
                pltpu.VMEM((tokens + 8, PAD), F32),
                pltpu.VMEM((tokens + 8, 128), F32),
                pltpu.VMEM((8, PAD), F32),
            ],
        ),
        out_shape=jax.ShapeDtypeStruct((tokens, PAD), BF),
        compiler_params=params(28),
        cost_estimate=pl.CostEstimate(
            flops=8_000_000_000, bytes_accessed=2_500_000, transcendentals=2_000_000
        ),
        name="scan",
    )(jnp.stack([position // 8, position % 8]).astype(jnp.int32), *operands, state)
    return out.reshape(16, rows, PAD)


def unpacked(back):
    return pl.pallas_call(
        unpack_kernel,
        out_shape=jax.ShapeDtypeStruct((2, back.shape[1], 8 * HD), BF),
        compiler_params=params(),
        name="unpack",
    )(back)


def after(values, done):
    return lax.optimization_barrier((values, done))[0]


def sent_home(one, two, three, axis):
    move = along(axis)
    return [move(one, 1), move(three, -1), move(two, 2)]


def per_device(
    group_queries, group_keys, group_values, cache_keys, cache_values, cache_lengths, mamba_x, mamba_bc,
    mamba_dt, conv_state_x, conv_state_bc, conv_weight_x, conv_bias_x, conv_weight_bc, conv_bias_bc,
    dt_bias, a_log, skip_d, ssm_state,
):
    position = lax.axis_index("ctx")
    info = cache_lengths
    queries = [group_queries[0], group_queries[1]]
    moves = [along("x"), along("y")]
    others = [[move(q, -1), move(q, 2), move(q, 1)] for q, move in zip(queries, moves)]
    packed, mine = channels_in(after(mamba_x, others[0][0]), mamba_bc, mamba_dt)
    first0, first1 = joined_rows(after(group_queries, packed), *others)
    far0, far1 = moves[1](first0, 2), moves[0](first1, 2)
    own0, own1, keys, values = attend(
        info, (0, 1), (0,), [first0, first1], None, None,
        (cache_keys, group_keys, cache_values, group_values),
    )
    first0, first1 = after((first0, first1), (far0, far1, own0))
    after0, before0 = moves[1](first0, -1), moves[1](first0, 1)
    after1, before1 = moves[0](first1, -1), moves[0](first1, 1)
    two0, two1 = attend(after(info, own0), (0, 1), (2,), [far0, far1], keys, values)
    scan_inputs = (
        mine, conv_state_x, conv_state_bc, conv_weight_x, conv_bias_x, conv_weight_bc, conv_bias_bc,
        dt_bias, a_log, skip_d, ssm_state,
    )
    scanned = state_space(position, *after(scan_inputs, two0))
    two0, two1 = after((two0, two1), (after0, before0, after1, before1))
    one0, three0, one1, three1 = attend(
        after(info, (two0, scanned)), (0, 1), (1, 3), [after0, before0, after1, before1], keys, values
    )
    back = lax.all_to_all(after(scanned, one0), "ctx", 0, 0, tiled=True)
    two0, two1 = moves[1](two0, 2), moves[0](two1, 2)
    side0 = [moves[1](one0, 1), moves[1](three0, -1)]
    three1 = after(three1, (two0, two1))
    side1 = [moves[0](one1, 1), moves[0](three1, -1)]
    blocks0 = merge([after(own0, scanned), *side0, two0])
    home0 = [blocks0[0], *sent_home(*blocks0[1:], "x")]
    blocks1 = merge([after(own1, blocks0[0]), *side1, two1])
    blocks1 = after(blocks1, back)
    home1 = [blocks1[0], *sent_home(*blocks1[1:], "y")]
    return finish(home0, home1), unpacked(back)


def solution(mesh):
    token = P("dp", "ctx", "head")
    placed = (
        token, token, token, token, token, P("dp"), token, P("dp", "ctx", None), token,
        P("dp", None, "head"), P("dp", None, None), P(None, "head"), P("head"), P(), P(),
        P("head"), P("head"), P("head"), P("dp", "head", None, None),
    )
    return jax.shard_map(
        per_device, mesh=mesh, in_specs=placed, out_specs=(token, token), check_vma=False
    )
```

```python
import functools
import math

import jax
import jax.numpy as jnp
from jax import lax
from jax.experimental import pallas as pl
from jax.experimental.pallas import tpu as pltpu
from jax.sharding import PartitionSpec as P

HD = 224
PAD = 256
L_LANE = 224
M_LANE = 226
NEG_FILL = -1e30
EMPTY_TOP = -8192.0
HIGHEST = lax.Precision.HIGHEST
BF = jnp.bfloat16
F32 = jnp.float32
SIDE = 4
MIB = 1024 * 1024


def params(mib=16):
    return pltpu.CompilerParams(vmem_limit_bytes=mib * MIB)


def shifted(value, dy, dx):
    pairs = [
        (y * SIDE + x, ((y + dy) % SIDE) * SIDE + (x + dx) % SIDE)
        for y in range(SIDE)
        for x in range(SIDE)
    ]
    return lax.ppermute(value, "ctx", pairs)


def along(axis):
    if axis == "x":
        return lambda value, step: shifted(value, 0, step)
    return lambda value, step: shifted(value, step, 0)


def widened(block, extra):
    return jnp.concatenate([block, extra], axis=1)


def pad_cache(info, request, k_ref, gk_ref, v_ref, gv_ref, ko_ref, vo_ref, h):
    rows = k_ref.shape[1]
    group_rows = gk_ref.shape[1]
    first = lax.axis_index("ctx") * rows
    length = info[request]
    lane = lax.broadcasted_iota(jnp.int32, (rows, PAD - HD), 1)
    row = lax.broadcasted_iota(jnp.int32, (rows, PAD - HD), 0)
    cache_bias = jnp.where((lane == 0) & (first + row >= length), NEG_FILL, 0.0).astype(BF)
    group_bias = jnp.zeros((group_rows, PAD - HD), BF)
    ones = jnp.where(lane == 0, 1.0, 0.0).astype(BF)
    window = slice(h * HD, (h + 1) * HD)
    ko_ref[0, h, :rows, :] = widened(k_ref[0, :, window], cache_bias)
    ko_ref[0, h, rows:, :] = widened(gk_ref[0, :, window], group_bias)
    vo_ref[0, h, :rows, :] = widened(v_ref[0, :, window], ones)
    vo_ref[0, h, rows:, :] = widened(gv_ref[0, :, window], ones[:group_rows])


def attend_kernel(requests, groups, pads, info, *refs):
    sets = len(groups)
    count = len(requests) * sets
    q_refs, refs = refs[:count], refs[count:]
    if pads:
        raw, refs = refs[:4], refs[4:]
        outs, (k_ref, v_ref) = refs[:count], refs[count:]
    else:
        (k_ref, v_ref), outs = refs[:2], refs[2:]
    turn = pl.program_id(0)
    here = k_ref.shape[1]
    span = q_refs[0].shape[0]
    rows = sets * span
    block = 64
    cached = k_ref.shape[2] - block
    scale = math.log2(math.e) / math.sqrt(HD)
    position = lax.axis_index("ctx")

    def body(n):
        row = lax.broadcasted_iota(jnp.int32, (block, block), 0)
        col = lax.broadcasted_iota(jnp.int32, (block, block), 1) + position * block
        masks = []
        for group in groups:
            for lap in range(SIDE):
                along_y, along_x = (group, lap) if requests[n] == 0 else (lap, group)
                source = ((position // SIDE + along_y) % SIDE) * SIDE + (position % SIDE + along_x) % SIDE
                masks.append(col <= row + source * block)
        allowed = jnp.concatenate(masks, axis=0)
        lane = lax.broadcasted_iota(jnp.int32, (rows, PAD), 1)
        mine = q_refs[n * sets : (n + 1) * sets]

        def scored(i):
            if pads:
                pad_cache(info, requests[n], *raw, k_ref, v_ref, i)
            queries = [ref[:, i * PAD : (i + 1) * PAD] for ref in mine]
            return lax.dot_general(
                jnp.concatenate(queries, axis=0) if sets > 1 else queries[0],
                k_ref[0, i],
                (((1,), (1,)), ((), ())),
                preferred_element_type=F32,
            )

        def store(i, scores):
            tail = jnp.where(allowed, scores[:, cached:], NEG_FILL)
            scores = jnp.concatenate([scores[:, :cached], tail], axis=1)
            top = jnp.maximum(jnp.max(scores, axis=1, keepdims=True) * scale, EMPTY_TOP)
            top = jnp.round(top).astype(BF).astype(F32)
            weights = jnp.exp2(scores * scale - top).astype(BF)
            out = jnp.dot(weights, v_ref[0, i], preferred_element_type=F32)
            out = jnp.where(lane == M_LANE, top, out).astype(BF)
            for at in range(sets):
                outs[n * sets + at][:, i * PAD : (i + 1) * PAD] = out[at * span : (at + 1) * span]

        scores = scored(0)
        for i in range(here):
            following = scored(i + 1) if i + 1 < here else None
            store(i, scores)
            scores = following

    for n in range(len(requests)):
        if len(requests) == 1:
            body(n)
        else:
            pl.when(turn == n)(functools.partial(body, n))


def attend(info, requests, groups, queries, keys, values, raw=None):
    sets = len(groups)
    span, width = queries[0].shape
    rows = sets * span
    heads = width // PAD
    steps = 2
    here = heads // steps
    if raw is None:
        _, _, total, _ = keys.shape
    else:
        _, cached, _ = raw[0].shape
        group_rows = raw[1].shape[1]
        total = cached + group_rows
    base = requests[0]

    def column(n):
        def at(r, g, s):
            return 0, jnp.where(r == n, g, jnp.where(r < n, 0, steps - 1))

        return at

    kv = pl.BlockSpec((1, here, total, PAD), lambda r, g, s: (base + r, g, 0, 0))
    order = [n for n in range(len(requests)) for _ in range(sets)]
    ins = [pl.BlockSpec((span, here * PAD), column(n)) for n in order]
    outs = [pl.BlockSpec((span, here * PAD), column(n)) for n in order]
    shapes = [jax.ShapeDtypeStruct((span, heads * PAD), BF)] * len(order)
    moved = 9_000_000 * len(requests) + 6 * len(requests) * rows * width
    if raw is None:
        operands, specs = [keys, values], [kv, kv]
    else:
        operands = list(raw)
        wide = pl.BlockSpec((1, cached, here * HD), lambda r, g, s: (r, 0, g))
        small = pl.BlockSpec((1, group_rows, here * HD), lambda r, g, s: (r, 0, g))
        specs = [wide, small, wide, small]
        outs += [kv, kv]
        shapes += [jax.ShapeDtypeStruct((len(requests), heads, total, PAD), BF)] * 2
        moved += 16_000_000
    work = len(requests) * heads * rows * total
    return pl.pallas_call(
        functools.partial(attend_kernel, requests, groups, raw is not None),
        grid_spec=pltpu.PrefetchScalarGridSpec(
            num_scalar_prefetch=1,
            grid=(len(requests), steps),
            in_specs=[*ins, *specs],
            out_specs=outs,
        ),
        out_shape=shapes,
        compiler_params=params(44 if raw is None and sets == 1 else 56),
        cost_estimate=pl.CostEstimate(flops=6 * work * PAD, bytes_accessed=moved, transcendentals=work),
        name="attend",
    )(info, *queries, *operands)


def join_kernel(own_ref, *refs):
    outs = refs[6:]
    rows = own_ref.shape[1]
    lane = lax.broadcasted_iota(jnp.int32, (rows, PAD - HD), 1)
    ones = jnp.where(lane == 0, 1.0, 0.0).astype(BF)
    for r, out in enumerate(outs):
        blocks = [own_ref.at[r], *refs[3 * r : 3 * r + 3]]
        for n, ref in enumerate(blocks):
            for h in range(own_ref.shape[2] // HD):
                out[n * rows : (n + 1) * rows, h * PAD : (h + 1) * PAD] = widened(
                    ref[:, h * HD : (h + 1) * HD], ones
                )


def joined_rows(own, others0, others1):
    _, rows, width = own.shape
    padded = width // HD * PAD
    return pl.pallas_call(
        join_kernel,
        out_shape=[jax.ShapeDtypeStruct((SIDE * rows, padded), BF)] * 2,
        compiler_params=params(),
        cost_estimate=pl.CostEstimate(flops=0, bytes_accessed=16 * rows * width * 2, transcendentals=0),
        name="join",
    )(own, *others0, *others1)


def merged(parts):
    tops = [part[:, M_LANE : M_LANE + 1] for part in parts]
    top = functools.reduce(jnp.maximum, tops)
    return sum(part * jnp.exp2(own - top) for part, own in zip(parts, tops)), top


def merge_kernel(*refs):
    parts, outs = refs[:4], refs[4:]
    rows = outs[0].shape[0]
    lane = lax.broadcasted_iota(jnp.int32, (rows, PAD), 1)
    for h in range(outs[0].shape[1] // PAD):
        window = slice(h * PAD, (h + 1) * PAD)
        for b in range(SIDE):
            at = slice(b * rows, (b + 1) * rows)
            total, top = merged([ref[at, window].astype(F32) for ref in parts])
            outs[b][:, window] = jnp.where(lane == M_LANE, top, total).astype(BF)


def merge(parts):
    rows, width = parts[0].shape
    steps = 2
    spec = pl.BlockSpec((rows, width // steps), lambda i: (0, i))
    out = pl.BlockSpec((rows // SIDE, width // steps), lambda i: (0, i))
    return pl.pallas_call(
        merge_kernel,
        grid=(steps,),
        in_specs=[spec] * 4,
        out_specs=[out] * 4,
        out_shape=[jax.ShapeDtypeStruct((rows // SIDE, width), BF)] * 4,
        compiler_params=params(56),
        cost_estimate=pl.CostEstimate(
            flops=rows * width * 8, bytes_accessed=rows * width * 10, transcendentals=0
        ),
        name="merge",
    )(*parts)


def finish_kernel(count, *refs):
    out_ref = refs[2 * count]
    heads = out_ref.shape[2] // HD
    for r in range(2):
        done = []
        for h in range(heads):
            window = slice(h * PAD, (h + 1) * PAD)
            total, _ = merged([ref[:, window].astype(F32) for ref in refs[r * count : (r + 1) * count]])
            done.append((total / total[:, L_LANE : L_LANE + 1])[:, :HD])
        out_ref[r] = jnp.concatenate(done, axis=1).astype(BF)


def finish(parts0, parts1):
    rows, width = parts0[0].shape
    heads = width // PAD
    return pl.pallas_call(
        functools.partial(finish_kernel, len(parts0)),
        out_shape=jax.ShapeDtypeStruct((2, rows, heads * HD), BF),
        compiler_params=params(),
        cost_estimate=pl.CostEstimate(
            flops=rows * width * 16, bytes_accessed=rows * width * 20, transcendentals=0
        ),
        name="finish",
    )(*parts0, *parts1)


def pack_kernel(x_ref, dt_ref, bc_ref, out_ref):
    rows = x_ref.shape[1]
    heads = dt_ref.shape[2]
    for r in range(2):
        extra = jnp.concatenate([dt_ref[r], jnp.zeros((rows, PAD - HD - heads), BF)], axis=1)
        for c in range(8):
            out_ref[r * 8 + c, :, :PAD] = jnp.concatenate(
                [x_ref[r, :, c * HD : (c + 1) * HD], extra], axis=1
            )
            out_ref[r * 8 + c, :, PAD:] = bc_ref[r]


def unpack_kernel(in_ref, out_ref):
    for r in range(2):
        out_ref[r] = jnp.concatenate(
            [in_ref[r * 8 + c].astype(F32)[:, :HD] for c in range(8)], axis=1
        ).astype(BF)


def split(value):
    high = value.astype(BF)
    return high, (value - high.astype(F32)).astype(BF)


def split_three(value):
    high = value.astype(BF)
    rest = value - high.astype(F32)
    middle, low = split(rest)
    return high, middle, low


def scan_kernel(
    info, data_ref, cx_ref, wx_ref, bx_ref, cb_ref, wb_ref, bb_ref, head_ref, state_ref, out_ref,
    xs_ref, bcs_ref, par_ref,
):
    tokens = data_ref.shape[0]
    chunk = 128
    request, start = info[0], info[1]
    first_head = (7 * start) // 2
    taps = wx_ref.shape[0]
    rim = taps - 1
    before = 8 - rim
    for c in range(8):

        @pl.when(start == c)
        def _():
            window = slice(c * HD, (c + 1) * HD)
            par_ref[0:taps, :HD] = wx_ref[:, window]
            par_ref[taps : taps + 1, :HD] = bx_ref[:, window]
            xs_ref[before:8, :HD] = cx_ref[request].astype(F32)[:, window]

    par_ref[:, HD:] = jnp.zeros((8, PAD - HD), F32)
    xs_ref[0:8, HD:] = jnp.zeros((8, PAD - HD), F32)
    bcs_ref[before:8, :] = cb_ref[request].astype(F32)
    xs_ref[8:, :] = data_ref[:, :PAD].astype(F32)
    bcs_ref[8:, :] = data_ref[:, PAD:].astype(F32)

    lane = lax.broadcasted_iota(jnp.int32, (8, PAD), 1) + start * HD
    head = lax.broadcasted_iota(jnp.int32, (8, PAD), 0) + first_head
    spread = (lane // 64 == head).astype(F32)
    spread3 = jnp.concatenate([spread] * 3, axis=0).astype(BF)
    pick = (
        lax.broadcasted_iota(jnp.int32, (128, 8), 0)
        == lax.broadcasted_iota(jnp.int32, (128, 8), 1) + (HD - 128) + first_head
    ).astype(F32)
    headpar = jnp.dot(head_ref[...], pick, precision=HIGHEST, preferred_element_type=F32)
    dt_bias, rate, skip = headpar[0:1], jnp.exp(headpar[1:2]), headpar[2:3]
    skip_wide = jnp.dot(skip, spread, precision=HIGHEST, preferred_element_type=F32)
    row = lax.broadcasted_iota(jnp.int32, (chunk, chunk), 0)
    col = lax.broadcasted_iota(jnp.int32, (chunk, chunk), 1)
    lower = row >= col
    lower_b = lower.astype(F32).astype(BF)
    pick_b = pick.astype(BF)
    masks = [spread[h : h + 1] for h in range(4)]
    state = jnp.concatenate(
        [state_ref[0, pl.ds(pl.multiple_of(start * HD, 32), HD), :], jnp.zeros((PAD - HD, 64), F32)], axis=0
    ).T
    for c in range(tokens // chunk):
        at = c * chunk
        x = jnp.zeros((chunk, PAD), F32) + par_ref[taps : taps + 1, :]
        bc = jnp.zeros((chunk, 128), F32) + bb_ref[...]
        for i in range(taps):
            x = x + par_ref[i : i + 1, :] * xs_ref[at + before + i : at + before + i + chunk, :]
            bc = bc + wb_ref[i : i + 1, :] * bcs_ref[at + before + i : at + before + i + chunk, :]
        x = x * jax.nn.sigmoid(x)
        bc = bc * jax.nn.sigmoid(bc)
        b, o = bc[:, :64], bc[:, 64:]
        raw = data_ref[at : at + chunk, 128:PAD]
        size = jnp.dot(raw, pick_b, preferred_element_type=F32) + dt_bias
        size = jnp.maximum(size, 0.0) + jnp.log1p(jnp.exp(-jnp.abs(size)))
        run = jnp.dot(
            lower_b, jnp.concatenate(split_three(-rate * size), axis=1), preferred_element_type=F32
        )
        run = run[:, :8] + run[:, 8:16] + run[:, 16:24]
        run_t = run.T
        wide = jnp.dot(
            jnp.concatenate(split_three(jnp.concatenate([size, run], axis=0)), axis=1),
            spread3,
            preferred_element_type=F32,
        )
        size_wide, run_wide = wide[:chunk], wide[chunk:]
        xdt = x * size_wide
        o_high, o_low = split(o)
        b_high, b_low = split(b)
        o_three = jnp.concatenate([o_high, o_high, o_low], axis=1)
        cross = lax.dot_general(
            o_three,
            jnp.concatenate([b_high, b_low, b_high], axis=1),
            (((1,), (1,)), ((), ())),
            preferred_element_type=F32,
        )
        pieces, mixes = [], []
        for h in range(4):
            gap = run[:, h : h + 1] - run_t[h : h + 1, :]
            mixes.append((jnp.exp(jnp.where(lower, gap, NEG_FILL)) * cross).astype(BF))
            pieces.append((xdt * masks[h]).astype(BF))
        y = jnp.dot(
            jnp.concatenate(mixes, axis=1), jnp.concatenate(pieces, axis=0), preferred_element_type=F32
        )
        s_high, s_low = split(state)
        y = y + jnp.exp(run_wide) * jnp.dot(
            o_three, jnp.concatenate([s_high, s_low, s_high], axis=0), preferred_element_type=F32
        )
        last = run_wide[chunk - 1 : chunk]
        w_high, w_low = split(xdt * jnp.exp(last - run_wide))
        state = state * jnp.exp(last) + lax.dot_general(
            jnp.concatenate([b_high, b_high, b_low], axis=0),
            jnp.concatenate([w_high, w_low, w_high], axis=0),
            (((0,), (0,)), ((), ())),
            preferred_element_type=F32,
        )
        out_ref[at : at + chunk, :] = (y + skip_wide * x).astype(BF)


def channels_in(mamba_x, mamba_bc, mamba_dt):
    rows = mamba_x.shape[1]
    packed = pl.pallas_call(
        pack_kernel,
        out_shape=jax.ShapeDtypeStruct((16, rows, PAD + 128), BF),
        compiler_params=params(),
        name="pack",
    )(mamba_x, mamba_dt, mamba_bc)
    return packed, lax.all_to_all(packed, "ctx", 0, 0, tiled=True).reshape(16 * rows, PAD + 128)


def state_space(
    position, mine, conv_state_x, conv_state_bc, conv_weight_x, conv_bias_x, conv_weight_bc,
    conv_bias_bc, dt_bias, a_log, skip_d, ssm_state,
):
    rows = mine.shape[0] // 16
    heads = dt_bias.shape[0]
    headpar = jnp.pad(jnp.stack([dt_bias, a_log, skip_d]), ((0, 5), (HD - 128, 128 - (HD - 128) - heads)))
    state = ssm_state.reshape(2, -1, 64)
    tokens = 16 * rows

    def whole(value):
        return pl.BlockSpec(value.shape, lambda i, s: (0,) * value.ndim)

    operands = (
        mine, conv_state_x, conv_weight_x, conv_bias_x[None], conv_state_bc, conv_weight_bc,
        conv_bias_bc[None], headpar,
    )
    out = pl.pallas_call(
        scan_kernel,
        grid_spec=pltpu.PrefetchScalarGridSpec(
            num_scalar_prefetch=1,
            grid=(1,),
            in_specs=[*map(whole, operands), pl.BlockSpec((1, *state.shape[1:]), lambda i, s: (s[0], 0, 0))],
            out_specs=pl.BlockSpec((tokens, PAD), lambda i, s: (0, 0)),
            scratch_shapes=[
                pltpu.VMEM((tokens + 8, PAD), F32),
                pltpu.VMEM((tokens + 8, 128), F32),
                pltpu.VMEM((8, PAD), F32),
            ],
        ),
        out_shape=jax.ShapeDtypeStruct((tokens, PAD), BF),
        compiler_params=params(28),
        cost_estimate=pl.CostEstimate(
            flops=8_000_000_000, bytes_accessed=2_500_000, transcendentals=2_000_000
        ),
        name="scan",
    )(jnp.stack([position // 8, position % 8]).astype(jnp.int32), *operands, state)
    return out.reshape(16, rows, PAD)


def unpacked(back):
    return pl.pallas_call(
        unpack_kernel,
        out_shape=jax.ShapeDtypeStruct((2, back.shape[1], 8 * HD), BF),
        compiler_params=params(),
        name="unpack",
    )(back)


def after(values, done):
    return lax.optimization_barrier((values, done))[0]


def sent_home(one, two, three, axis):
    move = along(axis)
    return [move(one, 1), move(three, -1), move(two, 2)]


def per_device(
    group_queries, group_keys, group_values, cache_keys, cache_values, cache_lengths, mamba_x, mamba_bc,
    mamba_dt, conv_state_x, conv_state_bc, conv_weight_x, conv_bias_x, conv_weight_bc, conv_bias_bc,
    dt_bias, a_log, skip_d, ssm_state,
):
    position = lax.axis_index("ctx")
    info = cache_lengths
    queries = [group_queries[0], group_queries[1]]
    moves = [along("x"), along("y")]
    others = [[move(q, -1), move(q, 2), move(q, 1)] for q, move in zip(queries, moves)]
    packed, mine = channels_in(after(mamba_x, others[0][0]), mamba_bc, mamba_dt)
    first0, first1 = joined_rows(after(group_queries, packed), *others)
    far0, far1 = moves[1](first0, 2), moves[0](first1, 2)
    own0, own1, keys, values = attend(
        info, (0, 1), (0,), [first0, first1], None, None,
        (cache_keys, group_keys, cache_values, group_values),
    )
    first0, first1 = after((first0, first1), (far0, far1, own0))
    after0, before0 = moves[1](first0, -1), moves[1](first0, 1)
    after1, before1 = moves[0](first1, -1), moves[0](first1, 1)
    two0, two1 = attend(after(info, own0), (0, 1), (2,), [far0, far1], keys, values)
    scan_inputs = (
        mine, conv_state_x, conv_state_bc, conv_weight_x, conv_bias_x, conv_weight_bc, conv_bias_bc,
        dt_bias, a_log, skip_d, ssm_state,
    )
    scanned = state_space(position, *after(scan_inputs, two0))
    two0, two1 = after((two0, two1), (after0, before0, after1, before1))
    one0, three0, one1, three1 = attend(
        after(info, (two0, scanned)), (0, 1), (1, 3), [after0, before0, after1, before1], keys, values
    )
    back = lax.all_to_all(after(scanned, one0), "ctx", 0, 0, tiled=True)
    two0, two1 = moves[1](two0, 2), moves[0](two1, 2)
    side0 = [moves[1](one0, 1), moves[1](three0, -1)]
    three1 = after(three1, (two0, two1))
    side1 = [moves[0](one1, 1), moves[0](three1, -1)]
    blocks0 = merge([after(own0, scanned), *side0, two0])
    home0 = [blocks0[0], *sent_home(*blocks0[1:], "x")]
    blocks1 = merge([after(own1, blocks0[0]), *side1, two1])
    blocks1 = after(blocks1, back)
    home1 = [blocks1[0], *sent_home(*blocks1[1:], "y")]
    return finish(home0, home1), unpacked(back)


def solution(mesh):
    token = P("dp", "ctx", "head")
    placed = (
        token, token, token, token, token, P("dp"), token, P("dp", "ctx", None), token,
        P("dp", None, "head"), P("dp", None, None), P(None, "head"), P("head"), P(), P(),
        P("head"), P("head"), P("head"), P("dp", "head", None, None),
    )
    return jax.shard_map(
        per_device, mesh=mesh, in_specs=placed, out_specs=(token, token), check_vma=False
    )
```
